32 devices in a mesh: exp: 4 (over z), tile: 8 (over y, x, core).
Axes of the slice: x: 2, y: 2, z: 4, core: 2. Of those that a mesh axis runs over, the one named last changes fastest.
Arguments:
- exposure: bfloat16 [4, 2048, 4096], P('exp', 'tile'), may hold values from -6 to 6
- row_taps: bfloat16 [3, 21], replicated, may hold values from -1.25 to 1.25
- column_taps: bfloat16 [3, 21], replicated, may hold values from -1.25 to 1.25
- basis_coef: float32 [4, 3], P('exp'), may hold values from -2.5 to 2.5
- warp_rows: bfloat16 [64, 128, 128], replicated, may hold values from -0.3 to 1.2
- warp_columns: bfloat16 [64, 128, 128], replicated, may hold values from -0.3 to 1.2
- warp_id: int32 [4, 8, 64], replicated, may hold values from 0 to 63
- route_device: int32 [4, 8, 64], replicated, may hold values from 0 to 31, as said below
- route_slot: int32 [4, 8, 64], replicated, may hold values from 0 to 63
- weight: float32 [4, 8], replicated, may hold values from 0.3 to 3
Outputs:
- coadd_patch: float32 [4096, 8192], P('exp', 'tile')
- difference: float32 [4, 2048, 4096], P('exp', 'tile')
The draws below stay inside these ranges and needn't reach their ends.
Inputs may be any that keep to these rules, and one draw needn't show every extreme that they name: `route_device`: the blocks of one device (its exposures of its tile, in order) name any one device at most 4 times, and some device is named exactly 4 times by the blocks of every device.
All inputs are finite; a program needn't handle non-finite values.
Results may differ from the reference program's by a relative error of at most 0.0058.
Values may be sent and summed in bfloat16 or wider, within the bound.
A program may use at most 128 MiB of HBM per device.

```python
import math
import jax
import jax.numpy as jnp
from jax import lax

BLOCK = 128
COLS = 4096
TILE_ROWS = 256
EXP_DEV = 1
TAPS = 21
HALF = 10
BASES = 3
WARPS = 64
SLOT_ROWS = 8
SLOT_COLS = 8
EXPOSURES = 4
HEIGHT = 2048
BLOCKS_TILE = 64
SLOTS = 64
CAP = 4
N_EXP = 4
N_TILE = 8


def lanczos_bank(key):
    shift_key, noise_key, dense_key = jax.random.split(key, 3)
    offsets = jax.random.uniform(shift_key, (WARPS,), minval=0.15, maxval=0.45)
    jitter = jax.random.uniform(noise_key, (WARPS, BLOCK, BLOCK), minval=0.9, maxval=1.1)
    dense_part = jnp.clip(0.04 * jax.random.normal(dense_key, (WARPS, BLOCK, BLOCK)), -0.1, 0.1)
    column_lag = (jnp.arange(BLOCK)[None, :] - jnp.arange(BLOCK)[:, None]).astype(jnp.float32)
    argument = column_lag[None, :, :] - offsets[:, None, None]
    kernel = jnp.sinc(argument) * jnp.sinc(argument / 3.0)
    inside = ((column_lag >= -2.0) & (column_lag <= 3.0)).astype(jnp.float32)
    return (kernel * inside[None, :, :] * jitter + dense_part).astype(jnp.bfloat16)


def draw_warp_rows(key, part):
    return lanczos_bank(jax.random.fold_in(key, 101))


def draw_warp_columns(key, part):
    return lanczos_bank(jax.random.fold_in(key, 202))


def draw_route_device(key, part):
    devices = N_EXP * N_TILE
    per_device = EXP_DEV * BLOCKS_TILE
    capacity = CAP
    keys_all = jax.random.split(jax.random.fold_in(key, 303), 5)
    hot_device = jax.random.randint(keys_all[0], (), 0, devices)
    others = jax.random.permutation(keys_all[1], devices - 1)
    remaining = per_device - capacity
    least_group = max(1, (remaining + devices - 2) // (devices - 1))
    group_size = jax.random.randint(keys_all[2], (devices, 1), least_group, capacity + 1)
    start_group = jax.random.randint(keys_all[3], (devices, 1), 0, devices - 1)
    orders = jax.vmap(lambda one_key: jax.random.permutation(one_key, per_device))(jax.random.split(keys_all[4], devices))
    later = jnp.maximum(orders - capacity, 0)
    group_index = (start_group + later // group_size) % (devices - 1)
    other_device = (hot_device + 1 + others[group_index]) % devices
    target = jnp.where(orders < capacity, hot_device, other_device).astype(jnp.int32)
    target = target.reshape(N_EXP, N_TILE, EXP_DEV, BLOCKS_TILE).transpose(0, 2, 1, 3)
    return target.reshape(EXP_DEV * N_EXP, N_TILE, BLOCKS_TILE)


def with_ends(result, stream_key, least, largest):
    extent = result.shape
    index_at = [jax.random.randint(jax.random.fold_in(stream_key, axis), (), 0, extent[axis]) for axis in range(len(extent))]
    result = result.at[tuple(index_at)].set(least)
    longest = extent.index(max(extent))
    index_at[longest] = (index_at[longest] + 1) % extent[longest]
    return result.at[tuple(index_at)].set(largest)


def block_scale(own_key, dims, cuts, least, high):
    def one(axis_at, blocks):
        steps = jax.random.uniform(jax.random.fold_in(jax.random.fold_in(own_key, 6), axis_at), (blocks,), jnp.float32, least / len(cuts), high / len(cuts))
        return jnp.repeat(jnp.exp(steps), dims[axis_at] // blocks).reshape((-1,) + (1,) * (len(dims) - axis_at - 1))

    factor_of = one(*cuts[0])
    for cut in cuts[1:]:
        factor_of = factor_of * one(*cut)
    return factor_of


def scatter_about(key, dims, spread, most, cuts=(), dtype=jnp.bfloat16):
    array = spread * jax.random.normal(key, dims, jnp.float32)
    if cuts:
        array = array * block_scale(key, dims, cuts, -0.22, 0.18)
    return jnp.clip(array, -most, most).astype(dtype)


def setup_inputs(seed: int = 0) -> dict:
    streams_of = jax.random.split(jax.random.key(seed), 11)
    exposure = scatter_about(streams_of[0], (EXPOSURES, HEIGHT, COLS), 1.0, 6.0, ((0, 4), (1, 8)))
    row_taps = scatter_about(streams_of[1], (BASES, TAPS), TAPS ** -0.5, 1.25)
    column_taps = scatter_about(streams_of[2], (BASES, TAPS), TAPS ** -0.5, 1.25)
    basis_coef = scatter_about(streams_of[3], (EXPOSURES, BASES), 0.6, 2.5, ((0, 4),), jnp.float32)
    warp_rows = draw_warp_rows(jax.random.fold_in(streams_of[10], 71), 0)
    warp_columns = draw_warp_columns(jax.random.fold_in(streams_of[10], 71), 0)
    warp_id = with_ends(jax.random.randint(streams_of[6], (EXPOSURES, N_TILE, BLOCKS_TILE), 0, WARPS), jax.random.fold_in(streams_of[6], 1), 0, WARPS - 1).astype(jnp.int32)
    route_device = draw_route_device(jax.random.fold_in(streams_of[10], 71), 0)
    route_slot = with_ends(jax.random.randint(streams_of[8], (EXPOSURES, N_TILE, BLOCKS_TILE), 0, SLOTS), jax.random.fold_in(streams_of[8], 1), 0, SLOTS - 1).astype(jnp.int32)
    weight = jnp.clip(jnp.exp(jax.random.uniform(streams_of[9], (EXPOSURES, N_TILE), jnp.float32, math.log(0.3), math.log(3.0))), 0.3, 3.0)
    return {"exposure": exposure, "row_taps": row_taps, "column_taps": column_taps, "basis_coef": basis_coef, "warp_rows": warp_rows, "warp_columns": warp_columns, "warp_id": warp_id, "route_device": route_device, "route_slot": route_slot, "weight": weight}


def shifted_sum(picture, tap_values, axis_index):
    padded = jnp.pad(picture, ((HALF, HALF), (0, 0)) if axis_index == 0 else ((0, 0), (HALF, HALF)))
    summed = jnp.zeros_like(picture)
    length = picture.shape[axis_index]
    for tap_index in range(TAPS):
        window = lax.slice_in_dim(padded, tap_index, tap_index + length, axis=axis_index)
        summed = summed + tap_values[tap_index] * window
    return summed


def match_kernel(picture, row_taps, column_taps, coef_row):
    values = picture.astype(jnp.float32)
    summed = jnp.zeros_like(values)
    for basis_idx in range(BASES):
        row_pass = (coef_row[basis_idx] * shifted_sum(values, row_taps[basis_idx].astype(jnp.float32), 0)).astype(jnp.bfloat16)
        row_pass = lax.optimization_barrier(row_pass).astype(jnp.float32)
        summed = summed + shifted_sum(row_pass, column_taps[basis_idx].astype(jnp.float32), 1)
    return summed


def reference(exposure, row_taps, column_taps, basis_coef, warp_rows, warp_columns, warp_id, route_device, route_slot, weight):
    row_blocks = TILE_ROWS // BLOCK
    col_blocks = COLS // BLOCK
    devices = N_EXP * N_TILE
    row_warps = warp_rows.astype(jnp.float32)
    col_warps = warp_columns.astype(jnp.float32)

    def forward(inputs):
        picture, coef_row, idents, tile_weight = inputs
        matched = match_kernel(picture, row_taps, column_taps, coef_row).astype(jnp.bfloat16)
        matched = lax.optimization_barrier(matched).astype(jnp.float32)
        pieces = matched.reshape(N_TILE, row_blocks, BLOCK, col_blocks, BLOCK).transpose(0, 1, 3, 2, 4)
        pieces = pieces.reshape(N_TILE * BLOCKS_TILE, BLOCK, BLOCK)
        flat_ids = idents.reshape(-1)
        first_pass = jnp.einsum("bij,bjc->bic", row_warps[flat_ids], pieces).astype(jnp.bfloat16)
        first_pass = lax.optimization_barrier(first_pass).astype(jnp.float32)
        second_pass = jnp.einsum("bic,bkc->bik", first_pass, col_warps[flat_ids])
        block_weight = jnp.repeat(tile_weight, BLOCKS_TILE)
        return (block_weight[:, None, None] * second_pass).astype(jnp.bfloat16)

    weighted = lax.map(forward, (exposure, basis_coef, warp_id, weight))
    weighted = lax.optimization_barrier(weighted)
    target_slot = (route_device * SLOTS + route_slot).reshape(-1).astype(jnp.int32)
    flat_weight = jnp.repeat(weight.reshape(-1), BLOCKS_TILE)
    numerator = jax.ops.segment_sum(weighted.reshape(-1, BLOCK * BLOCK).astype(jnp.float32), target_slot, num_segments=devices * SLOTS)
    denominator = jax.ops.segment_sum(flat_weight, target_slot, num_segments=devices * SLOTS)
    coadd_slots = numerator / jnp.maximum(denominator, 1.0)[:, None]
    coadd_patch = coadd_slots.reshape(N_EXP, N_TILE, SLOT_ROWS, SLOT_COLS, BLOCK, BLOCK).transpose(0, 2, 4, 1, 3, 5)
    coadd_patch = coadd_patch.reshape(N_EXP * SLOT_ROWS * BLOCK, N_TILE * SLOT_COLS * BLOCK)
    templates = coadd_slots.astype(jnp.bfloat16)[target_slot].reshape(EXPOSURES, N_TILE * BLOCKS_TILE, BLOCK, BLOCK)

    def backward(inputs):
        picture, coef_row, idents, pieces = inputs
        flat_ids = idents.reshape(-1)
        pieces = lax.optimization_barrier(pieces).astype(jnp.float32)
        first_pass = jnp.einsum("bji,bjc->bic", row_warps[flat_ids], pieces).astype(jnp.bfloat16)
        first_pass = lax.optimization_barrier(first_pass).astype(jnp.float32)
        unwarped = jnp.einsum("bic,bck->bik", first_pass, col_warps[flat_ids]).astype(jnp.bfloat16)
        template_image = unwarped.reshape(N_TILE, row_blocks, col_blocks, BLOCK, BLOCK).transpose(0, 1, 3, 2, 4)
        template_image = lax.optimization_barrier(template_image.reshape(HEIGHT, COLS))
        return picture.astype(jnp.float32) - match_kernel(template_image, row_taps, column_taps, coef_row)

    difference = lax.map(backward, (exposure, basis_coef, warp_id, templates))
    return coadd_patch, difference
```

```python
import functools

import jax
import jax.numpy as jnp
from jax import lax
from jax.experimental import pallas as pl
from jax.experimental.pallas import tpu as pltpu
from jax.sharding import PartitionSpec as P

BLOCK = 128
HALF = 10
RIM = 16
WIDE = 2 * BLOCK
SLOT_ROWS = 8
SLOT_COLS = 8
VMEM_BYTES = 56 * 1024 * 1024


def halo(image, axis):
    count = lax.axis_size(axis)
    forward = [(i, i + 1) for i in range(count - 1)]
    backward = [(target, source) for source, target in forward]
    above = lax.ppermute(image[-RIM:], axis, forward)
    below = lax.ppermute(image[:RIM], axis, backward)
    return above, below


def banded(taps, rows, cols, offset, transposed):
    shape = (rows, cols)
    lag = lax.broadcasted_iota(jnp.int32, shape, 1) - lax.broadcasted_iota(jnp.int32, shape, 0)
    lag = lag - offset
    if transposed:
        lag = lag.T
    count = taps.shape[1]
    hit = lag[None, :, :] == jnp.arange(count, dtype=jnp.int32)[:, None, None]
    picked = jnp.where(hit[None], taps[:, :, None, None], jnp.zeros((), taps.dtype))
    return jnp.sum(picked.astype(jnp.float32), axis=1).astype(jnp.bfloat16)


def row_stage(coef, above, image, below, row_bands, padded, passes):
    bases = passes.shape[0]
    rows, cols = image.shape
    blocks = rows // BLOCK
    span = BLOCK + 2 * RIM
    padded[:RIM, :] = above[...]
    padded[RIM : RIM + rows, :] = image[...]
    padded[RIM + rows :, :] = below[...]
    edge = jnp.zeros((rows, BLOCK), passes.dtype)
    for basis in range(bases):
        passes[basis, :, :BLOCK] = edge
        passes[basis, :, BLOCK + cols :] = edge

    def step(at, carry):
        start = pl.multiple_of(at * WIDE, WIDE)
        for block in range(blocks):
            top = block * BLOCK
            sums = jnp.dot(
                row_bands[...],
                padded[top : top + span, pl.ds(start, WIDE)],
                preferred_element_type=jnp.float32,
            )
            for basis in range(bases):
                scaled = coef[0, basis] * sums[basis * BLOCK : (basis + 1) * BLOCK]
                passes[basis, top : top + BLOCK, pl.ds(start + BLOCK, WIDE)] = scaled.astype(
                    passes.dtype
                )
        return carry

    lax.fori_loop(0, cols // WIDE, step, 0, unroll=2)


def column_chunk(passes, column_bands, start):
    total = None
    for basis in range(passes.shape[0]):
        term = jnp.dot(
            passes[basis, :, pl.ds(start, 2 * WIDE)],
            column_bands[basis],
            preferred_element_type=jnp.float32,
        )
        total = term if total is None else total + term
    return total


def forward_kernel(
    coef, ident, place, weight, above, image, below, row_bands, column_bands, warp_rows,
    warp_columns, packed, padded, passes,
):
    rows, cols = image.shape
    blocks = rows // BLOCK
    across = cols // BLOCK
    row_stage(coef, above, image, below, row_bands, padded, passes)
    blank = jnp.zeros((BLOCK, BLOCK), packed.dtype)

    def clear(at, carry):
        packed[at] = blank
        return carry

    lax.fori_loop(0, packed.shape[0], clear, 0, unroll=4)
    scale = weight[0]

    def step(at, carry):
        start = pl.multiple_of(at * WIDE, WIDE)
        matched = column_chunk(passes, column_bands, start).astype(jnp.bfloat16)
        for block in range(blocks):
            for side in range(WIDE // BLOCK):
                number = block * across + at * (WIDE // BLOCK) + side
                which = ident[number]
                piece = matched[
                    block * BLOCK : (block + 1) * BLOCK, side * BLOCK : (side + 1) * BLOCK
                ]
                first = jnp.dot(
                    warp_rows[which], piece, preferred_element_type=jnp.float32
                ).astype(jnp.bfloat16)
                second = lax.dot_general(
                    first,
                    warp_columns[which],
                    (((1,), (1,)), ((), ())),
                    preferred_element_type=jnp.float32,
                )
                packed[place[number]] = (scale * second).astype(packed.dtype)
        return carry

    lax.fori_loop(0, cols // WIDE, step, 0, unroll=2)


def coadd_kernel(slot, valid, inverse, arrived, patch, picked):
    side = SLOT_COLS * BLOCK
    blank = jnp.zeros((BLOCK, side), jnp.float32)
    for row in range(SLOT_ROWS):
        patch[row * BLOCK : (row + 1) * BLOCK, :] = blank

    def where(number):
        top = pl.multiple_of((number // SLOT_COLS) * BLOCK, BLOCK)
        left = pl.multiple_of((number % SLOT_COLS) * BLOCK, BLOCK)
        return pl.ds(top, BLOCK), pl.ds(left, BLOCK)

    def add(at, carry):
        @pl.when(valid[at] != 0)
        def _():
            spot = where(slot[at])
            patch[spot] = patch[spot] + arrived[at].astype(jnp.float32)

        return carry

    lax.fori_loop(0, arrived.shape[0], add, 0)

    def divide(at, carry):
        spot = where(at)
        patch[spot] = patch[spot] * inverse[at]
        return carry

    lax.fori_loop(0, SLOT_ROWS * SLOT_COLS, divide, 0, unroll=4)

    def pick(at, carry):
        picked[at] = patch[where(slot[at])].astype(picked.dtype)
        return carry

    lax.fori_loop(0, arrived.shape[0], pick, 0, unroll=4)


def unwarp_kernel(ident, place, returned, warp_rows, warp_columns, image):
    rows, cols = image.shape
    blocks = rows // BLOCK
    across = cols // BLOCK

    def step(at, carry):
        start = pl.multiple_of(at * WIDE, WIDE)
        for block in range(blocks):
            for side in range(WIDE // BLOCK):
                number = block * across + at * (WIDE // BLOCK) + side
                which = ident[number]
                back = lax.dot_general(
                    warp_rows[which],
                    returned[place[number]],
                    (((0,), (0,)), ((), ())),
                    preferred_element_type=jnp.float32,
                ).astype(jnp.bfloat16)
                piece = jnp.dot(back, warp_columns[which], preferred_element_type=jnp.float32)
                image[
                    block * BLOCK : (block + 1) * BLOCK, pl.ds(start + side * BLOCK, BLOCK)
                ] = piece.astype(image.dtype)
        return carry

    lax.fori_loop(0, cols // WIDE, step, 0, unroll=2)


def difference_kernel(
    coef, above, image, below, row_bands, column_bands, exposure, difference, padded, passes
):
    cols = image.shape[1]
    row_stage(coef, above, image, below, row_bands, padded, passes)

    def step(at, carry):
        start = pl.multiple_of(at * WIDE, WIDE)
        matched = column_chunk(passes, column_bands, start)
        spot = pl.ds(start, WIDE)
        difference[:, spot] = exposure[:, spot].astype(jnp.float32) - matched
        return carry

    lax.fori_loop(0, cols // WIDE, step, 0, unroll=2)


def scalars(count):
    return [pl.BlockSpec(memory_space=pltpu.SMEM)] * count


def vectors(count):
    return [pl.BlockSpec(memory_space=pltpu.VMEM)] * count


def shards(
    exposure, row_taps, column_taps, basis_coef, warp_rows, warp_columns, warp_id, route_device,
    route_slot, weight,
):
    n_exp = lax.axis_size("exp")
    n_tile = lax.axis_size("tile")
    devices = n_exp * n_tile
    rows, cols = exposure.shape[1:]
    bases = row_taps.shape[0]
    blocks = (rows // BLOCK) * (cols // BLOCK)
    capacity = max(2, (2 * blocks + devices - 1) // devices)
    slots = SLOT_ROWS * SLOT_COLS
    buffered = devices * capacity
    myself = lax.axis_index("exp") * n_tile + lax.axis_index("tile")
    params = pltpu.CompilerParams(vmem_limit_bytes=VMEM_BYTES)
    mine = exposure[0]

    above, below = halo(mine, "tile")
    row_bands = banded(row_taps, BLOCK, BLOCK + 2 * RIM, RIM - HALF, False)
    row_bands = row_bands.reshape(bases * BLOCK, BLOCK + 2 * RIM)
    column_bands = banded(column_taps, WIDE, 2 * WIDE, BLOCK - HALF, True)

    dest_all = route_device.reshape(devices, blocks)
    slot_all = route_slot.reshape(devices, blocks)
    weight_all = weight.reshape(devices)
    earlier = jnp.arange(blocks)[:, None] > jnp.arange(blocks)[None, :]
    same = dest_all[:, :, None] == dest_all[:, None, :]
    rank_all = jnp.sum(same & earlier[None], axis=2, dtype=jnp.int32)
    place_all = dest_all * capacity + rank_all
    place = lax.dynamic_index_in_dim(place_all, myself, 0, keepdims=False)
    ident = lax.dynamic_index_in_dim(warp_id.reshape(devices, blocks), myself, 0, keepdims=False)
    my_weight = lax.dynamic_index_in_dim(weight_all, myself, 0, keepdims=True)
    hit = (dest_all[:, None, :] == myself) & (
        rank_all[:, None, :] == jnp.arange(capacity, dtype=jnp.int32)[None, :, None]
    )
    slot = jnp.sum(jnp.where(hit, slot_all[:, None, :], 0), axis=2, dtype=jnp.int32)
    slot = slot.reshape(buffered)
    valid = jnp.any(hit, axis=2).reshape(buffered).astype(jnp.int32)
    owned = (slot_all[None] == jnp.arange(slots, dtype=jnp.int32)[:, None, None]) & (
        dest_all == myself
    )[None]
    total = jnp.sum(jnp.where(owned, weight_all[None, :, None], 0.0), axis=(1, 2))
    inverse = 1.0 / jnp.maximum(total, 1.0)

    work = [
        pltpu.VMEM((rows + 2 * RIM, cols), jnp.bfloat16),
        pltpu.VMEM((bases, rows, cols + 2 * BLOCK), jnp.bfloat16),
    ]
    packed = pl.pallas_call(
        forward_kernel,
        out_shape=jax.ShapeDtypeStruct((buffered, BLOCK, BLOCK), jnp.bfloat16),
        in_specs=scalars(4) + vectors(7),
        out_specs=pl.BlockSpec(memory_space=pltpu.VMEM),
        scratch_shapes=work,
        compiler_params=params,
    )(
        basis_coef, ident, place, my_weight, above, mine, below, row_bands, column_bands,
        warp_rows, warp_columns,
    )
    packed = packed.reshape(devices, capacity, BLOCK, BLOCK)
    arrived = lax.all_to_all(packed, ("exp", "tile"), split_axis=0, concat_axis=0, tiled=True)
    patch, picked = pl.pallas_call(
        coadd_kernel,
        out_shape=(
            jax.ShapeDtypeStruct((SLOT_ROWS * BLOCK, SLOT_COLS * BLOCK), jnp.float32),
            jax.ShapeDtypeStruct((buffered, BLOCK, BLOCK), jnp.bfloat16),
        ),
        in_specs=scalars(3) + vectors(1),
        out_specs=tuple(vectors(2)),
        compiler_params=params,
    )(slot, valid, inverse, arrived.reshape(buffered, BLOCK, BLOCK))
    picked = picked.reshape(devices, capacity, BLOCK, BLOCK)
    returned = lax.all_to_all(picked, ("exp", "tile"), split_axis=0, concat_axis=0, tiled=True)
    template = pl.pallas_call(
        unwarp_kernel,
        out_shape=jax.ShapeDtypeStruct((rows, cols), jnp.bfloat16),
        in_specs=scalars(2) + vectors(3),
        out_specs=pl.BlockSpec(memory_space=pltpu.VMEM),
        compiler_params=params,
    )(ident, place, returned.reshape(buffered, BLOCK, BLOCK), warp_rows, warp_columns)
    template_above, template_below = halo(template, "tile")
    difference = pl.pallas_call(
        difference_kernel,
        out_shape=jax.ShapeDtypeStruct((rows, cols), jnp.float32),
        in_specs=scalars(1) + vectors(6),
        out_specs=pl.BlockSpec(memory_space=pltpu.VMEM),
        scratch_shapes=work,
        compiler_params=params,
    )(
        basis_coef, template_above, template, template_below, row_bands, column_bands, mine
    )
    return patch, difference[None]


def solution(mesh):
    placed = (P("exp", "tile", None), P(), P(), P("exp", None), P(), P(), P(), P(), P(), P())
    return jax.shard_map(
        shards,
        mesh=mesh,
        in_specs=placed,
        out_specs=(P("exp", "tile"), P("exp", "tile", None)),
        check_vma=False,
    )
```

```python
import functools

import jax
import jax.numpy as jnp
from jax import lax
from jax.experimental import pallas as pl
from jax.experimental.pallas import tpu as pltpu
from jax.sharding import PartitionSpec as P

BLOCK = 128
HALF = 10
RIM = 16
WIDE = 2 * BLOCK
SLOT_ROWS = 8
SLOT_COLS = 8
VMEM_BYTES = 56 * 1024 * 1024


def halo(image, axis):
    count = lax.axis_size(axis)
    forward = [(i, i + 1) for i in range(count - 1)]
    backward = [(target, source) for source, target in forward]
    above = lax.ppermute(image[-RIM:], axis, forward)
    below = lax.ppermute(image[:RIM], axis, backward)
    return above, below


def banded(taps, rows, cols, offset):
    shape = (rows, cols)
    lag = lax.broadcasted_iota(jnp.int32, shape, 1) - lax.broadcasted_iota(jnp.int32, shape, 0)
    lag = lag - offset
    count = taps.shape[1]
    total = jnp.zeros((taps.shape[0], rows, cols), jnp.float32)
    for tap in range(count):
        value = taps[:, tap, None, None].astype(jnp.float32)
        total = total + jnp.where(lag == tap, value, 0.0)
    return total.astype(jnp.bfloat16)


def banded_transposed(taps, rows, cols, offset):
    shape = (rows, cols)
    lag = lax.broadcasted_iota(jnp.int32, shape, 0) - lax.broadcasted_iota(jnp.int32, shape, 1)
    lag = lag - offset
    count = taps.shape[1]
    total = jnp.zeros((taps.shape[0], rows, cols), jnp.float32)
    for tap in range(count):
        value = taps[:, tap, None, None].astype(jnp.float32)
        total = total + jnp.where(lag == tap, value, 0.0)
    return total.astype(jnp.bfloat16)


def row_stage(coef, above, image, below, row_bands, column_bands, padded, passes, bands):
    bases = passes.shape[0]
    rows, cols = image.shape
    blocks = rows // BLOCK
    span = BLOCK + 2 * RIM
    padded[:RIM, :] = above[...]
    padded[RIM : RIM + rows, :] = image[...]
    padded[RIM + rows :, :] = below[...]
    edge = jnp.zeros((rows, BLOCK), passes.dtype)
    bands[...] = jnp.zeros_like(bands)
    for side in range(WIDE // BLOCK):
        top = side * BLOCK
        bands[:, top : top + 3 * BLOCK, top : top + BLOCK] = column_bands[...]
    for basis in range(bases):
        passes[basis, :, :BLOCK] = edge
        passes[basis, :, BLOCK + cols :] = edge

    def step(at, carry):
        start = pl.multiple_of(at * WIDE, WIDE)
        for block in range(blocks):
            top = block * BLOCK
            sums = jnp.dot(
                row_bands[...],
                padded[top : top + span, pl.ds(start, WIDE)],
                preferred_element_type=jnp.float32,
            )
            for basis in range(bases):
                scaled = coef[0, basis] * sums[basis * BLOCK : (basis + 1) * BLOCK]
                passes[basis, top : top + BLOCK, pl.ds(start + BLOCK, WIDE)] = scaled.astype(
                    passes.dtype
                )
        return carry

    lax.fori_loop(0, cols // WIDE, step, 0, unroll=2)


def column_chunk(passes, column_bands, start):
    total = None
    for basis in range(passes.shape[0]):
        term = jnp.dot(
            passes[basis, :, pl.ds(start, 2 * WIDE)],
            column_bands[basis],
            preferred_element_type=jnp.float32,
        )
        total = term if total is None else total + term
    return total


def match_kernel(
    coef, above, image, below, row_bands, column_bands, matched, padded, passes, bands
):
    rows, cols = image.shape
    blocks = rows // BLOCK
    across = cols // BLOCK
    row_stage(coef, above, image, below, row_bands, column_bands, padded, passes, bands)
    matched[blocks * across] = jnp.zeros((BLOCK, BLOCK), matched.dtype)

    def step(at, carry):
        start = pl.multiple_of(at * WIDE, WIDE)
        chunk = column_chunk(passes, bands, start).astype(matched.dtype)
        for block in range(blocks):
            for side in range(WIDE // BLOCK):
                number = block * across + at * (WIDE // BLOCK) + side
                matched[number] = chunk[
                    block * BLOCK : (block + 1) * BLOCK, side * BLOCK : (side + 1) * BLOCK
                ]
        return carry

    lax.fori_loop(0, cols // WIDE, step, 0, unroll=2)


def partner(me, step, devices):
    sign = 2 * lax.rem(step, 2) - 1
    shift = devices // 2 + sign * lax.div(step + 1, 2)
    return lax.rem(me + shift, devices), lax.rem(me + devices - shift, devices)


def address(device, n_tile):
    return (lax.div(device, n_tile), lax.rem(device, n_tile))


def greet(me, devices, n_tile):
    barrier = pltpu.get_barrier_semaphore()

    def hello(step, carry):
        other = lax.rem(me + step + 1, devices)
        pl.semaphore_signal(
            barrier, inc=1, device_id=address(other, n_tile), device_id_type=pl.DeviceIdType.MESH
        )
        return carry

    lax.fori_loop(0, devices - 1, hello, 0)
    pl.semaphore_wait(barrier, devices - 1)


def transfer(source, target, me, other, capacity, n_tile, send_sem, recv_sem):
    return pltpu.make_async_remote_copy(
        src_ref=source.at[pl.ds(other * capacity, capacity)],
        dst_ref=target.at[pl.ds(me * capacity, capacity)],
        send_sem=send_sem.at[other],
        recv_sem=recv_sem.at[me],
        device_id=address(other, n_tile),
        device_id_type=pl.DeviceIdType.MESH,
    )


def receipt(source, target, other, capacity, n_tile, send_sem, recv_sem):
    return pltpu.make_async_remote_copy(
        src_ref=source.at[pl.ds(other * capacity, capacity)],
        dst_ref=target.at[pl.ds(other * capacity, capacity)],
        send_sem=send_sem.at[other],
        recv_sem=recv_sem.at[other],
        device_id=address(other, n_tile),
        device_id_type=pl.DeviceIdType.MESH,
    )


def send_kernel(
    n_exp, n_tile, source, ident, weight, matched, warp_rows, warp_columns, arrived, packed,
    send_sem, recv_sem,
):
    devices = n_exp * n_tile
    capacity = packed.shape[0] // devices
    me = lax.axis_index("exp") * n_tile + lax.axis_index("tile")
    greet(me, devices, n_tile)
    scale = weight[0]

    def warp(other, target):
        for rank in range(capacity):
            spot = other * capacity + rank
            which = ident[spot]
            first = jnp.dot(
                warp_rows[which], matched[source[spot]], preferred_element_type=jnp.float32
            ).astype(jnp.bfloat16)
            second = lax.dot_general(
                first,
                warp_columns[which],
                (((1,), (1,)), ((), ())),
                preferred_element_type=jnp.float32,
            )
            target[spot] = (scale * second).astype(target.dtype)

    def step(at, carry):
        other, _ = partner(me, at, devices)
        warp(other, packed)
        transfer(packed, arrived, me, other, capacity, n_tile, send_sem, recv_sem).start()
        return carry

    lax.fori_loop(0, devices - 1, step, 0)
    warp(me, arrived)

    def finish(at, carry):
        _, other = partner(me, at, devices)
        receipt(packed, arrived, other, capacity, n_tile, send_sem, recv_sem).wait()
        return carry

    lax.fori_loop(0, devices - 1, finish, 0)


def return_kernel(
    n_exp, n_tile, ident, place, picked, warp_rows, warp_columns, image, returned, unwarped,
    send_sem, recv_sem,
):
    devices = n_exp * n_tile
    capacity = picked.shape[0] // devices
    across = image.shape[1] // BLOCK
    me = lax.axis_index("exp") * n_tile + lax.axis_index("tile")
    greet(me, devices, n_tile)

    def begin(at, carry):
        other, _ = partner(me, at, devices)
        transfer(picked, returned, me, other, capacity, n_tile, send_sem, recv_sem).start()
        return carry

    lax.fori_loop(0, devices - 1, begin, 0)

    def unwarp(other, origin):
        for rank in range(capacity):
            spot = other * capacity + rank
            which = ident[spot]
            back = lax.dot_general(
                warp_rows[which],
                origin[spot],
                (((0,), (0,)), ((), ())),
                preferred_element_type=jnp.float32,
            ).astype(jnp.bfloat16)
            piece = jnp.dot(back, warp_columns[which], preferred_element_type=jnp.float32)
            unwarped[spot] = piece.astype(unwarped.dtype)

    unwarp(me, picked)

    def finish(at, carry):
        _, other = partner(me, at, devices)
        receipt(picked, returned, other, capacity, n_tile, send_sem, recv_sem).wait()
        unwarp(other, returned)
        return carry

    lax.fori_loop(0, devices - 1, finish, 0)

    def gather(at, carry):
        left = pl.multiple_of(at * BLOCK, BLOCK)
        for block in range(image.shape[0] // BLOCK):
            image[block * BLOCK : (block + 1) * BLOCK, pl.ds(left, BLOCK)] = unwarped[
                place[block * across + at]
            ]
        return carry

    lax.fori_loop(0, across, gather, 0)


def coadd_kernel(slot, valid, inverse, arrived, patch, picked):
    side = SLOT_COLS * BLOCK
    blank = jnp.zeros((BLOCK, side), jnp.float32)
    for row in range(SLOT_ROWS):
        patch[row * BLOCK : (row + 1) * BLOCK, :] = blank

    def where(number):
        top = pl.multiple_of((number // SLOT_COLS) * BLOCK, BLOCK)
        left = pl.multiple_of((number % SLOT_COLS) * BLOCK, BLOCK)
        return pl.ds(top, BLOCK), pl.ds(left, BLOCK)

    def add(at, carry):
        @pl.when(valid[at] != 0)
        def _():
            spot = where(slot[at])
            patch[spot] = patch[spot] + arrived[at].astype(jnp.float32)

        return carry

    lax.fori_loop(0, arrived.shape[0], add, 0)

    def divide(at, carry):
        spot = where(at)
        patch[spot] = patch[spot] * inverse[at]
        return carry

    lax.fori_loop(0, SLOT_ROWS * SLOT_COLS, divide, 0, unroll=4)

    def pick(at, carry):
        picked[at] = patch[where(slot[at])].astype(picked.dtype)
        return carry

    lax.fori_loop(0, arrived.shape[0], pick, 0, unroll=4)


def difference_kernel(
    coef, above, image, below, row_bands, column_bands, exposure, difference, padded, passes,
    bands,
):
    cols = image.shape[1]
    row_stage(coef, above, image, below, row_bands, column_bands, padded, passes, bands)

    def step(at, carry):
        start = pl.multiple_of(at * WIDE, WIDE)
        matched = column_chunk(passes, bands, start)
        spot = pl.ds(start, WIDE)
        difference[:, spot] = exposure[:, spot].astype(jnp.float32) - matched
        return carry

    lax.fori_loop(0, cols // WIDE, step, 0, unroll=2)


def scalars(count):
    return [pl.BlockSpec(memory_space=pltpu.SMEM)] * count


def vectors(count):
    return [pl.BlockSpec(memory_space=pltpu.VMEM)] * count


def shards(
    exposure, row_taps, column_taps, basis_coef, warp_rows, warp_columns, warp_id, route_device,
    route_slot, weight,
):
    n_exp = lax.axis_size("exp")
    n_tile = lax.axis_size("tile")
    devices = n_exp * n_tile
    rows, cols = exposure.shape[1:]
    bases = row_taps.shape[0]
    blocks = (rows // BLOCK) * (cols // BLOCK)
    capacity = max(2, (2 * blocks + devices - 1) // devices)
    slots = SLOT_ROWS * SLOT_COLS
    buffered = devices * capacity
    myself = lax.axis_index("exp") * n_tile + lax.axis_index("tile")
    params = pltpu.CompilerParams(vmem_limit_bytes=VMEM_BYTES)
    mine = exposure[0]

    above, below = halo(mine, "tile")
    row_bands = banded(row_taps, BLOCK, BLOCK + 2 * RIM, RIM - HALF)
    row_bands = row_bands.reshape(bases * BLOCK, BLOCK + 2 * RIM)
    column_bands = banded_transposed(column_taps, 3 * BLOCK, BLOCK, BLOCK - HALF)

    dest_all = route_device.reshape(devices, blocks)
    slot_all = route_slot.reshape(devices, blocks)
    weight_all = weight.reshape(devices)
    earlier = jnp.arange(blocks)[:, None] > jnp.arange(blocks)[None, :]
    same = dest_all[:, :, None] == dest_all[:, None, :]
    rank_all = jnp.sum(same & earlier[None], axis=2, dtype=jnp.int32)
    place_all = dest_all * capacity + rank_all
    place = lax.dynamic_index_in_dim(place_all, myself, 0, keepdims=False)
    ident = lax.dynamic_index_in_dim(warp_id.reshape(devices, blocks), myself, 0, keepdims=False)
    taken = place[None, :] == jnp.arange(buffered, dtype=jnp.int32)[:, None]
    source = jnp.min(
        jnp.where(taken, jnp.arange(blocks, dtype=jnp.int32)[None, :], blocks), axis=1
    )
    spot_ident = jnp.sum(jnp.where(taken, ident[None, :], 0), axis=1, dtype=jnp.int32)
    my_weight = lax.dynamic_index_in_dim(weight_all, myself, 0, keepdims=True)
    hit = (dest_all[:, None, :] == myself) & (
        rank_all[:, None, :] == jnp.arange(capacity, dtype=jnp.int32)[None, :, None]
    )
    slot = jnp.sum(jnp.where(hit, slot_all[:, None, :], 0), axis=2, dtype=jnp.int32)
    slot = slot.reshape(buffered)
    valid = jnp.any(hit, axis=2).reshape(buffered).astype(jnp.int32)
    owned = (slot_all[None] == jnp.arange(slots, dtype=jnp.int32)[:, None, None]) & (
        dest_all == myself
    )[None]
    total = jnp.sum(jnp.where(owned, weight_all[None, :, None], 0.0), axis=(1, 2))
    inverse = 1.0 / jnp.maximum(total, 1.0)

    work = [
        pltpu.VMEM((rows + 2 * RIM, cols), jnp.bfloat16),
        pltpu.VMEM((bases, rows, cols + 2 * BLOCK), jnp.bfloat16),
        pltpu.VMEM((bases, 2 * WIDE, WIDE), jnp.bfloat16),
    ]
    semaphores = [pltpu.SemaphoreType.DMA((devices,)), pltpu.SemaphoreType.DMA((devices,))]
    buffer = jax.ShapeDtypeStruct((buffered, BLOCK, BLOCK), jnp.bfloat16)
    matched = pl.pallas_call(
        match_kernel,
        out_shape=jax.ShapeDtypeStruct((blocks + 1, BLOCK, BLOCK), jnp.bfloat16),
        in_specs=scalars(1) + vectors(5),
        out_specs=pl.BlockSpec(memory_space=pltpu.VMEM),
        scratch_shapes=work,
        compiler_params=params,
    )(basis_coef, above, mine, below, row_bands, column_bands)
    arrived = pl.pallas_call(
        functools.partial(send_kernel, n_exp, n_tile),
        out_shape=buffer,
        in_specs=scalars(3) + vectors(3),
        out_specs=pl.BlockSpec(memory_space=pltpu.VMEM),
        scratch_shapes=[pltpu.VMEM(buffer.shape, buffer.dtype)] + semaphores,
        compiler_params=pltpu.CompilerParams(
            vmem_limit_bytes=VMEM_BYTES, collective_id=0, has_side_effects=True
        ),
    )(source, spot_ident, my_weight, matched, warp_rows, warp_columns)
    patch, picked = pl.pallas_call(
        coadd_kernel,
        out_shape=(
            jax.ShapeDtypeStruct((SLOT_ROWS * BLOCK, SLOT_COLS * BLOCK), jnp.float32),
            buffer,
        ),
        in_specs=scalars(3) + vectors(1),
        out_specs=tuple(vectors(2)),
        compiler_params=params,
    )(slot, valid, inverse, arrived)
    template = pl.pallas_call(
        functools.partial(return_kernel, n_exp, n_tile),
        out_shape=jax.ShapeDtypeStruct((rows, cols), jnp.bfloat16),
        in_specs=scalars(2) + vectors(3),
        out_specs=pl.BlockSpec(memory_space=pltpu.VMEM),
        scratch_shapes=[pltpu.VMEM(buffer.shape, buffer.dtype)] * 2 + semaphores,
        compiler_params=pltpu.CompilerParams(
            vmem_limit_bytes=VMEM_BYTES, collective_id=1, has_side_effects=True
        ),
    )(spot_ident, place, picked, warp_rows, warp_columns)
    template_above, template_below = halo(template, "tile")
    difference = pl.pallas_call(
        difference_kernel,
        out_shape=jax.ShapeDtypeStruct((rows, cols), jnp.float32),
        in_specs=scalars(1) + vectors(6),
        out_specs=pl.BlockSpec(memory_space=pltpu.VMEM),
        scratch_shapes=work,
        compiler_params=params,
    )(
        basis_coef, template_above, template, template_below, row_bands, column_bands, mine
    )
    return patch, difference[None]


def solution(mesh):
    placed = (P("exp", "tile", None), P(), P(), P("exp", None), P(), P(), P(), P(), P(), P())
    return jax.shard_map(
        shards,
        mesh=mesh,
        in_specs=placed,
        out_specs=(P("exp", "tile"), P("exp", "tile", None)),
        check_vma=False,
    )
```

```python
import functools

import jax
import jax.numpy as jnp
from jax import lax
from jax.experimental import pallas as pl
from jax.experimental.pallas import tpu as pltpu
from jax.sharding import PartitionSpec as P

BLOCK = 128
HALF = 10
RIM = 16
WIDE = 2 * BLOCK
SLOT_ROWS = 8
SLOT_COLS = 8
VMEM_BYTES = 56 * 1024 * 1024


def halo(image, axis):
    count = lax.axis_size(axis)
    forward = [(i, i + 1) for i in range(count - 1)]
    backward = [(target, source) for source, target in forward]
    above = lax.ppermute(image[-RIM:], axis, forward)
    below = lax.ppermute(image[:RIM], axis, backward)
    return above, below


def banded(taps, rows, cols, offset):
    shape = (rows, cols)
    lag = lax.broadcasted_iota(jnp.int32, shape, 1) - lax.broadcasted_iota(jnp.int32, shape, 0)
    lag = lag - offset
    count = taps.shape[1]
    total = jnp.zeros((taps.shape[0], rows, cols), jnp.float32)
    for tap in range(count):
        value = taps[:, tap, None, None].astype(jnp.float32)
        total = total + jnp.where(lag == tap, value, 0.0)
    return total.astype(jnp.bfloat16)


def banded_transposed(taps, rows, cols, offset):
    shape = (rows, cols)
    lag = lax.broadcasted_iota(jnp.int32, shape, 0) - lax.broadcasted_iota(jnp.int32, shape, 1)
    lag = lag - offset
    count = taps.shape[1]
    total = jnp.zeros((taps.shape[0], rows, cols), jnp.float32)
    for tap in range(count):
        value = taps[:, tap, None, None].astype(jnp.float32)
        total = total + jnp.where(lag == tap, value, 0.0)
    return total.astype(jnp.bfloat16)


def row_stage(coef, above, image, below, row_bands, column_bands, padded, passes, bands):
    bases = passes.shape[0]
    rows, cols = image.shape
    blocks = rows // BLOCK
    span = BLOCK + 2 * RIM
    padded[:RIM, :] = above[...]
    padded[RIM : RIM + rows, :] = image[...]
    padded[RIM + rows :, :] = below[...]
    edge = jnp.zeros((rows, BLOCK), passes.dtype)
    bands[...] = jnp.zeros_like(bands)
    for side in range(WIDE // BLOCK):
        top = side * BLOCK
        bands[:, top : top + 3 * BLOCK, top : top + BLOCK] = column_bands[...]
    for basis in range(bases):
        passes[basis, :, :BLOCK] = edge
        passes[basis, :, BLOCK + cols :] = edge

    def step(at, carry):
        start = pl.multiple_of(at * WIDE, WIDE)
        for block in range(blocks):
            top = block * BLOCK
            sums = jnp.dot(
                row_bands[...],
                padded[top : top + span, pl.ds(start, WIDE)],
                preferred_element_type=jnp.float32,
            )
            for basis in range(bases):
                scaled = coef[0, basis] * sums[basis * BLOCK : (basis + 1) * BLOCK]
                passes[basis, top : top + BLOCK, pl.ds(start + BLOCK, WIDE)] = scaled.astype(
                    passes.dtype
                )
        return carry

    lax.fori_loop(0, cols // WIDE, step, 0, unroll=2)


def column_chunk(passes, column_bands, start):
    total = None
    for basis in range(passes.shape[0]):
        term = jnp.dot(
            passes[basis, :, pl.ds(start, 2 * WIDE)],
            column_bands[basis],
            preferred_element_type=jnp.float32,
        )
        total = term if total is None else total + term
    return total


def match_kernel(
    capacity, coef, route, warp_id, above, image, below, row_bands, column_bands, matched, place,
    source, ident, padded, passes, bands, count,
):
    rows, cols = image.shape
    me = lax.axis_index("exp") * lax.axis_size("tile") + lax.axis_index("tile")

    def clear(at, carry):
        count[at] = 0
        for rank in range(capacity):
            source[at * capacity + rank] = route.shape[1]
            ident[at * capacity + rank] = 0
        return carry

    lax.fori_loop(0, route.shape[0], clear, 0)

    def assign(at, carry):
        device = route[me, at]
        rank = count[device]
        count[device] = rank + 1
        spot = device * capacity + rank
        place[at] = spot
        source[spot] = at
        ident[spot] = warp_id[me, at]
        return carry

    lax.fori_loop(0, route.shape[1], assign, 0)
    blocks = rows // BLOCK
    across = cols // BLOCK
    row_stage(coef, above, image, below, row_bands, column_bands, padded, passes, bands)
    matched[blocks * across] = jnp.zeros((BLOCK, BLOCK), matched.dtype)

    def step(at, carry):
        start = pl.multiple_of(at * WIDE, WIDE)
        chunk = column_chunk(passes, bands, start).astype(matched.dtype)
        for block in range(blocks):
            for side in range(WIDE // BLOCK):
                number = block * across + at * (WIDE // BLOCK) + side
                matched[number] = chunk[
                    block * BLOCK : (block + 1) * BLOCK, side * BLOCK : (side + 1) * BLOCK
                ]
        return carry

    lax.fori_loop(0, cols // WIDE, step, 0, unroll=2)


def partner(me, step, devices):
    half = devices // 2
    pair = lax.div(step, 2)
    odd = lax.rem(pair, 2)
    far = half + (2 * odd - 1) * lax.div(pair + 1, 2)
    near = (1 - odd) * (1 + lax.div(pair, 2)) + odd * (devices - 1 - lax.div(pair, 2))
    turn = lax.rem(step, 2)
    shift = (1 - turn) * far + turn * near
    return lax.rem(me + shift, devices), lax.rem(me + devices - shift, devices)


def address(device, n_tile):
    return (lax.div(device, n_tile), lax.rem(device, n_tile))


def greet(me, devices, n_tile):
    barrier = pltpu.get_barrier_semaphore()

    def hello(step, carry):
        other = lax.rem(me + step + 1, devices)
        pl.semaphore_signal(
            barrier, inc=1, device_id=address(other, n_tile), device_id_type=pl.DeviceIdType.MESH
        )
        return carry

    lax.fori_loop(0, devices - 1, hello, 0)
    pl.semaphore_wait(barrier, devices - 1)


def transfer(source, target, me, other, capacity, n_tile, send_sem, recv_sem):
    return pltpu.make_async_remote_copy(
        src_ref=source.at[pl.ds(other * capacity, capacity)],
        dst_ref=target.at[pl.ds(me * capacity, capacity)],
        send_sem=send_sem.at[other],
        recv_sem=recv_sem.at[me],
        device_id=address(other, n_tile),
        device_id_type=pl.DeviceIdType.MESH,
    )


def receipt(source, target, other, capacity, n_tile, send_sem, recv_sem):
    return pltpu.make_async_remote_copy(
        src_ref=source.at[pl.ds(other * capacity, capacity)],
        dst_ref=target.at[pl.ds(other * capacity, capacity)],
        send_sem=send_sem.at[other],
        recv_sem=recv_sem.at[other],
        device_id=address(other, n_tile),
        device_id_type=pl.DeviceIdType.MESH,
    )


def send_kernel(
    n_exp, n_tile, source, ident, weight, matched, warp_rows, warp_columns, route, slot, arrived,
    table, packed, send_sem, recv_sem,
):
    devices = n_exp * n_tile
    capacity = packed.shape[0] // devices
    me = lax.axis_index("exp") * n_tile + lax.axis_index("tile")
    greet(me, devices, n_tile)
    scale = weight[lax.axis_index("exp"), lax.axis_index("tile")]

    def warp(other, target):
        for rank in range(capacity):
            spot = other * capacity + rank
            which = ident[spot]
            first = jnp.dot(
                warp_rows[which], matched[source[spot]], preferred_element_type=jnp.float32
            ).astype(jnp.bfloat16)
            second = lax.dot_general(
                first,
                warp_columns[which],
                (((1,), (1,)), ((), ())),
                preferred_element_type=jnp.float32,
            )
            target[spot] = (scale * second).astype(target.dtype)

    def step(at, carry):
        other, _ = partner(me, at, devices)
        warp(other, packed)
        transfer(packed, arrived, me, other, capacity, n_tile, send_sem, recv_sem).start()
        return carry

    lax.fori_loop(0, devices - 1, step, 0)
    warp(me, arrived)

    count = route.shape[1]
    hit = route[...] == me
    later = (
        lax.broadcasted_iota(jnp.int32, (count, count), 0)
        < lax.broadcasted_iota(jnp.int32, (count, count), 1)
    )
    rank_of = jnp.dot(
        hit.astype(jnp.float32), later.astype(jnp.float32), preferred_element_type=jnp.float32
    ).astype(jnp.int32)
    column = lax.broadcasted_iota(jnp.int32, table.shape, 1)
    filled = jnp.zeros(table.shape, jnp.int32)
    none = SLOT_ROWS * SLOT_COLS
    for rank in range(capacity):
        chosen = jnp.where(hit & (rank_of == rank), slot[...] - none, 0)
        found = jnp.sum(chosen, axis=1, keepdims=True) + none
        filled = jnp.where(column == rank, found, filled)
    table[...] = filled

    def finish(at, carry):
        _, other = partner(me, at, devices)
        receipt(packed, arrived, other, capacity, n_tile, send_sem, recv_sem).wait()
        return carry

    lax.fori_loop(0, devices - 1, finish, 0)


def return_kernel(
    n_exp, n_tile, ident, place, table, value, warp_rows, warp_columns, image, picked, returned,
    unwarped, send_sem, recv_sem,
):
    devices = n_exp * n_tile
    capacity = picked.shape[0] // devices
    across = image.shape[1] // BLOCK
    me = lax.axis_index("exp") * n_tile + lax.axis_index("tile")
    greet(me, devices, n_tile)

    def pick(other):
        for rank in range(capacity):
            picked[other * capacity + rank] = value[table[other, rank]]

    def begin(at, carry):
        other, _ = partner(me, at, devices)
        pick(other)
        transfer(picked, returned, me, other, capacity, n_tile, send_sem, recv_sem).start()
        return carry

    lax.fori_loop(0, devices - 1, begin, 0)

    def unwarp(other, origin):
        for rank in range(capacity):
            spot = other * capacity + rank
            which = ident[spot]
            back = lax.dot_general(
                warp_rows[which],
                origin[spot],
                (((0,), (0,)), ((), ())),
                preferred_element_type=jnp.float32,
            ).astype(jnp.bfloat16)
            piece = jnp.dot(back, warp_columns[which], preferred_element_type=jnp.float32)
            unwarped[spot] = piece.astype(unwarped.dtype)

    pick(me)
    unwarp(me, picked)

    def finish(at, carry):
        _, other = partner(me, at, devices)
        receipt(picked, returned, other, capacity, n_tile, send_sem, recv_sem).wait()
        unwarp(other, returned)
        return carry

    lax.fori_loop(0, devices - 1, finish, 0)

    def gather(at, carry):
        left = pl.multiple_of(at * BLOCK, BLOCK)
        for block in range(image.shape[0] // BLOCK):
            image[block * BLOCK : (block + 1) * BLOCK, pl.ds(left, BLOCK)] = unwarped[
                place[block * across + at]
            ]
        return carry

    lax.fori_loop(0, across, gather, 0)


def coadd_kernel(n_tile, table, weight, arrived, patch, value, sums, total):
    slots = SLOT_ROWS * SLOT_COLS
    capacity = arrived.shape[0] // table.shape[0]
    blank = jnp.zeros((BLOCK, BLOCK), jnp.float32)

    def clear(at, carry):
        sums[at] = blank
        total[at] = 0.0
        return carry

    lax.fori_loop(0, slots + 1, clear, 0, unroll=5)

    def add(at, carry):
        share = weight[lax.div(at, n_tile), lax.rem(at, n_tile)]
        for rank in range(capacity):
            slot = table[at, rank]
            sums[slot] = sums[slot] + arrived[at * capacity + rank].astype(jnp.float32)
            total[slot] = total[slot] + share
        return carry

    lax.fori_loop(0, table.shape[0], add, 0, unroll=2)

    def divide(at, carry):
        for column in range(SLOT_COLS):
            number = at * SLOT_COLS + column
            weights = jnp.maximum(jnp.full((1, BLOCK), total[number], jnp.float32), 1.0)
            mean = sums[number] * (1.0 / weights)
            patch[
                pl.ds(pl.multiple_of(at * BLOCK, BLOCK), BLOCK),
                column * BLOCK : (column + 1) * BLOCK,
            ] = mean
            value[number] = mean.astype(value.dtype)
        return carry

    lax.fori_loop(0, SLOT_ROWS, divide, 0)
    value[slots] = blank.astype(value.dtype)


def difference_kernel(
    coef, above, image, below, row_bands, column_bands, exposure, difference, padded, passes,
    bands,
):
    cols = image.shape[1]
    row_stage(coef, above, image, below, row_bands, column_bands, padded, passes, bands)

    def step(at, carry):
        start = pl.multiple_of(at * WIDE, WIDE)
        matched = column_chunk(passes, bands, start)
        spot = pl.ds(start, WIDE)
        difference[:, spot] = exposure[:, spot].astype(jnp.float32) - matched
        return carry

    lax.fori_loop(0, cols // WIDE, step, 0, unroll=2)


def scalars(count):
    return [pl.BlockSpec(memory_space=pltpu.SMEM)] * count


def vectors(count):
    return [pl.BlockSpec(memory_space=pltpu.VMEM)] * count


def shards(
    exposure, row_taps, column_taps, basis_coef, warp_rows, warp_columns, warp_id, route_device,
    route_slot, weight,
):
    n_exp = lax.axis_size("exp")
    n_tile = lax.axis_size("tile")
    devices = n_exp * n_tile
    rows, cols = exposure.shape[1:]
    bases = row_taps.shape[0]
    blocks = (rows // BLOCK) * (cols // BLOCK)
    capacity = max(2, (2 * blocks + devices - 1) // devices)
    buffered = devices * capacity
    params = pltpu.CompilerParams(vmem_limit_bytes=VMEM_BYTES)
    mine = exposure[0]

    above, below = halo(mine, "tile")
    row_bands = banded(row_taps, BLOCK, BLOCK + 2 * RIM, RIM - HALF)
    row_bands = row_bands.reshape(bases * BLOCK, BLOCK + 2 * RIM)
    column_bands = banded_transposed(column_taps, 3 * BLOCK, BLOCK, BLOCK - HALF)

    route = route_device.reshape(devices, blocks)
    slot = route_slot.reshape(devices, blocks)

    work = [
        pltpu.VMEM((rows + 2 * RIM, cols), jnp.bfloat16),
        pltpu.VMEM((bases, rows, cols + 2 * BLOCK), jnp.bfloat16),
        pltpu.VMEM((bases, 2 * WIDE, WIDE), jnp.bfloat16),
    ]
    semaphores = [pltpu.SemaphoreType.DMA((devices,)), pltpu.SemaphoreType.DMA((devices,))]
    buffer = jax.ShapeDtypeStruct((buffered, BLOCK, BLOCK), jnp.bfloat16)
    matched, place, source, ident = pl.pallas_call(
        functools.partial(match_kernel, capacity),
        out_shape=(
            jax.ShapeDtypeStruct((blocks + 1, BLOCK, BLOCK), jnp.bfloat16),
            jax.ShapeDtypeStruct((blocks,), jnp.int32),
            jax.ShapeDtypeStruct((buffered,), jnp.int32),
            jax.ShapeDtypeStruct((buffered,), jnp.int32),
        ),
        in_specs=scalars(3) + vectors(5),
        out_specs=tuple(vectors(1) + scalars(3)),
        scratch_shapes=work + [pltpu.SMEM((devices,), jnp.int32)],
        compiler_params=params,
    )(
        basis_coef, route, warp_id.reshape(devices, blocks), above, mine, below, row_bands,
        column_bands,
    )
    arrived, table = pl.pallas_call(
        functools.partial(send_kernel, n_exp, n_tile),
        out_shape=(buffer, jax.ShapeDtypeStruct((devices, capacity), jnp.int32)),
        in_specs=scalars(3) + vectors(5),
        out_specs=tuple(vectors(2)),
        scratch_shapes=[pltpu.VMEM(buffer.shape, buffer.dtype)] + semaphores,
        compiler_params=pltpu.CompilerParams(
            vmem_limit_bytes=VMEM_BYTES, collective_id=0, has_side_effects=True
        ),
    )(source, ident, weight, matched, warp_rows, warp_columns, route, slot)
    patch, value = pl.pallas_call(
        functools.partial(coadd_kernel, n_tile),
        out_shape=(
            jax.ShapeDtypeStruct((SLOT_ROWS * BLOCK, SLOT_COLS * BLOCK), jnp.float32),
            jax.ShapeDtypeStruct((SLOT_ROWS * SLOT_COLS + 1, BLOCK, BLOCK), jnp.bfloat16),
        ),
        in_specs=scalars(2) + vectors(1),
        out_specs=tuple(vectors(2)),
        scratch_shapes=[
            pltpu.VMEM((SLOT_ROWS * SLOT_COLS + 1, BLOCK, BLOCK), jnp.float32),
            pltpu.SMEM((SLOT_ROWS * SLOT_COLS + 1,), jnp.float32),
        ],
        compiler_params=params,
    )(table, weight, arrived)
    template = pl.pallas_call(
        functools.partial(return_kernel, n_exp, n_tile),
        out_shape=jax.ShapeDtypeStruct((rows, cols), jnp.bfloat16),
        in_specs=scalars(3) + vectors(3),
        out_specs=pl.BlockSpec(memory_space=pltpu.VMEM),
        scratch_shapes=[pltpu.VMEM(buffer.shape, buffer.dtype)] * 3 + semaphores,
        compiler_params=pltpu.CompilerParams(
            vmem_limit_bytes=VMEM_BYTES, collective_id=1, has_side_effects=True
        ),
    )(ident, place, table, value, warp_rows, warp_columns)
    template_above, template_below = halo(template, "tile")
    difference = pl.pallas_call(
        difference_kernel,
        out_shape=jax.ShapeDtypeStruct((rows, cols), jnp.float32),
        in_specs=scalars(1) + vectors(6),
        out_specs=pl.BlockSpec(memory_space=pltpu.VMEM),
        scratch_shapes=work,
        compiler_params=params,
    )(
        basis_coef, template_above, template, template_below, row_bands, column_bands, mine
    )
    return patch, difference[None]


def solution(mesh):
    placed = (P("exp", "tile", None), P(), P(), P("exp", None), P(), P(), P(), P(), P(), P())
    return jax.shard_map(
        shards,
        mesh=mesh,
        in_specs=placed,
        out_specs=(P("exp", "tile"), P("exp", "tile", None)),
        check_vma=False,
    )
```

```python
import functools

import jax
import jax.numpy as jnp
from jax import lax
from jax.experimental import pallas as pl
from jax.experimental.pallas import tpu as pltpu
from jax.sharding import PartitionSpec as P

BLOCK = 128
HALF = 10
RIM = 16
WIDE = 2 * BLOCK
SLOT_ROWS = 8
SLOT_COLS = 8


def edge_copies(image, above, below, send_sem, recv_sem):
    rows = image.shape[0]
    row, tile, count = lax.axis_index("exp"), lax.axis_index("tile"), lax.axis_size("tile")
    onward = pltpu.make_async_remote_copy(
        src_ref=image.at[pl.ds(rows - RIM, RIM)],
        dst_ref=above,
        send_sem=send_sem.at[0],
        recv_sem=recv_sem.at[0],
        device_id=(row, lax.rem(tile + 1, count)),
        device_id_type=pl.DeviceIdType.MESH,
    )
    backward = pltpu.make_async_remote_copy(
        src_ref=image.at[pl.ds(0, RIM)],
        dst_ref=below,
        send_sem=send_sem.at[1],
        recv_sem=recv_sem.at[1],
        device_id=(row, lax.rem(tile + count - 1, count)),
        device_id_type=pl.DeviceIdType.MESH,
    )
    return onward, backward


def start_edges(image, above, below, send_sem, recv_sem):
    tile, count = lax.axis_index("tile"), lax.axis_size("tile")
    onward, backward = edge_copies(image, above, below, send_sem, recv_sem)

    @pl.when(tile < count - 1)
    def _():
        onward.start()

    @pl.when(tile > 0)
    def _():
        backward.start()

    @pl.when(tile == 0)
    def _():
        above[...] = jnp.zeros_like(above)

    @pl.when(tile == count - 1)
    def _():
        below[...] = jnp.zeros_like(below)


def finish_edges(image, above, below, send_sem, recv_sem):
    tile, count = lax.axis_index("tile"), lax.axis_size("tile")
    onward, backward = edge_copies(image, above, below, send_sem, recv_sem)

    @pl.when(tile < count - 1)
    def _():
        onward.wait_send()
        backward.wait_recv()

    @pl.when(tile > 0)
    def _():
        backward.wait_send()
        onward.wait_recv()


def banded(taps, basis, lag):
    total = jnp.zeros(lag.shape, jnp.float32)
    for tap in range(taps.shape[1]):
        value = jnp.broadcast_to(taps[basis : basis + 1, tap : tap + 1], lag.shape)
        total = jnp.where(lag == tap, value, total)
    return total.astype(jnp.bfloat16)


def ranked(hit):
    count = hit.shape[1]
    later = (
        lax.broadcasted_iota(jnp.int32, (count, count), 0)
        < lax.broadcasted_iota(jnp.int32, (count, count), 1)
    )
    ranks = jnp.dot(
        hit.astype(jnp.float32), later.astype(jnp.float32), preferred_element_type=jnp.float32
    )
    return ranks.astype(jnp.int32)


def by_rank(hit, ranks, values, none, shape):
    column = lax.broadcasted_iota(jnp.int32, shape, 1)
    filled = jnp.zeros(shape, jnp.int32)
    for rank in range(shape[1]):
        chosen = jnp.where(hit & (ranks == rank), values - none, 0)
        filled = jnp.where(column == rank, jnp.sum(chosen, axis=1, keepdims=True) + none, filled)
    return filled


def prepare_kernel(
    image, row_taps, column_taps, route, warp_id, above, below, row_bands, bands, source, ident,
    place, send_sem, recv_sem,
):
    row, tile, count = lax.axis_index("exp"), lax.axis_index("tile"), lax.axis_size("tile")
    me = row * count + tile
    barrier = pltpu.get_barrier_semaphore()

    @pl.when(tile < count - 1)
    def _():
        pl.semaphore_signal(
            barrier, inc=1, device_id=(row, lax.rem(tile + 1, count)),
            device_id_type=pl.DeviceIdType.MESH,
        )

    @pl.when(tile > 0)
    def _():
        pl.semaphore_signal(
            barrier, inc=1, device_id=(row, lax.rem(tile + count - 1, count)),
            device_id_type=pl.DeviceIdType.MESH,
        )

    bases = row_taps.shape[0]
    taps = row_taps[...].astype(jnp.float32)
    shape = (BLOCK, BLOCK + 2 * RIM)
    lag = lax.broadcasted_iota(jnp.int32, shape, 1) - lax.broadcasted_iota(jnp.int32, shape, 0)
    for basis in range(bases):
        row_bands[basis * BLOCK : (basis + 1) * BLOCK, :] = banded(
            taps, basis, lag - (RIM - HALF)
        )

    peers = jnp.minimum(tile, 1) + jnp.minimum(count - 1 - tile, 1)
    pl.semaphore_wait(barrier, peers)

    start_edges(image, above, below, send_sem, recv_sem)

    taps = column_taps[...].astype(jnp.float32)
    shape = (3 * BLOCK, BLOCK)
    lag = lax.broadcasted_iota(jnp.int32, shape, 0) - lax.broadcasted_iota(jnp.int32, shape, 1)
    bands[...] = jnp.zeros_like(bands)
    for basis in range(bases):
        band = banded(taps, basis, lag - (BLOCK - HALF))
        for side in range(WIDE // BLOCK):
            top = side * BLOCK
            bands[basis, top : top + 3 * BLOCK, top : top + BLOCK] = band

    devices, blocks = route.shape
    capacity = source.shape[1]
    device = lax.broadcasted_iota(jnp.int32, (devices, blocks), 0)
    hit = jnp.broadcast_to(route[pl.ds(me, 1), :], (devices, blocks)) == device
    ranks = ranked(hit)
    number = lax.broadcasted_iota(jnp.int32, (devices, blocks), 1)
    source[...] = by_rank(hit, ranks, number, blocks, source.shape)
    mine = jnp.broadcast_to(warp_id[pl.ds(me, 1), :], (devices, blocks))
    ident[...] = by_rank(hit, ranks, mine, 0, ident.shape)
    place[...] = jnp.sum(jnp.where(hit, device * capacity + ranks, 0), axis=0, keepdims=True)

    finish_edges(image, above, below, send_sem, recv_sem)


def row_stage(coef, above, image, below, row_bands, padded, passes):
    bases = passes.shape[0]
    rows, cols = image.shape
    blocks = rows // BLOCK
    span = BLOCK + 2 * RIM
    padded[:RIM, :] = above[...]
    padded[RIM : RIM + rows, :] = image[...]
    padded[RIM + rows :, :] = below[...]
    edge = jnp.zeros((rows, BLOCK), passes.dtype)
    for basis in range(bases):
        passes[basis, :, :BLOCK] = edge
        passes[basis, :, BLOCK + cols :] = edge

    def step(at, carry):
        start = pl.multiple_of(at * WIDE, WIDE)
        for block in range(blocks):
            top = block * BLOCK
            sums = jnp.dot(
                row_bands[...],
                padded[top : top + span, pl.ds(start, WIDE)],
                preferred_element_type=jnp.float32,
            )
            for basis in range(bases):
                scaled = coef[0, basis] * sums[basis * BLOCK : (basis + 1) * BLOCK]
                passes[basis, top : top + BLOCK, pl.ds(start + BLOCK, WIDE)] = scaled.astype(
                    passes.dtype
                )
        return carry

    lax.fori_loop(0, cols // WIDE, step, 0, unroll=2)


def column_chunk(passes, column_bands, start):
    total = None
    for basis in range(passes.shape[0]):
        term = jnp.dot(
            passes[basis, :, pl.ds(start, 2 * WIDE)],
            column_bands[basis],
            preferred_element_type=jnp.float32,
        )
        total = term if total is None else total + term
    return total


def match_kernel(coef, above, image, below, row_bands, bands, matched, padded, passes):
    rows, cols = image.shape
    blocks = rows // BLOCK
    across = cols // BLOCK
    row_stage(coef, above, image, below, row_bands, padded, passes)
    matched[blocks * across] = jnp.zeros((BLOCK, BLOCK), matched.dtype)

    def step(at, carry):
        start = pl.multiple_of(at * WIDE, WIDE)
        chunk = column_chunk(passes, bands, start).astype(matched.dtype)
        for block in range(blocks):
            for side in range(WIDE // BLOCK):
                number = block * across + at * (WIDE // BLOCK) + side
                matched[number] = chunk[
                    block * BLOCK : (block + 1) * BLOCK, side * BLOCK : (side + 1) * BLOCK
                ]
        return carry

    lax.fori_loop(0, cols // WIDE, step, 0, unroll=2)


def partner(me, step, devices):
    half = devices // 2
    pair = lax.div(step, 2)
    odd = lax.rem(pair, 2)
    far = half + (2 * odd - 1) * lax.div(pair + 1, 2)
    near = (1 - odd) * (1 + lax.div(pair, 2)) + odd * (devices - 1 - lax.div(pair, 2))
    turn = lax.rem(step, 2)
    shift = (1 - turn) * far + turn * near
    return lax.rem(me + shift, devices), lax.rem(me + devices - shift, devices)


def address(device, n_tile):
    return (lax.div(device, n_tile), lax.rem(device, n_tile))


def greet(me, devices, n_tile):
    barrier = pltpu.get_barrier_semaphore()

    def hello(step, carry):
        other = lax.rem(me + step + 1, devices)
        pl.semaphore_signal(
            barrier, inc=1, device_id=address(other, n_tile), device_id_type=pl.DeviceIdType.MESH
        )
        return carry

    lax.fori_loop(0, devices - 1, hello, 0)
    pl.semaphore_wait(barrier, devices - 1)


def transfer(source, target, me, other, capacity, n_tile, send_sem, recv_sem):
    return pltpu.make_async_remote_copy(
        src_ref=source.at[pl.ds(other * capacity, capacity)],
        dst_ref=target.at[pl.ds(me * capacity, capacity)],
        send_sem=send_sem.at[other],
        recv_sem=recv_sem.at[me],
        device_id=address(other, n_tile),
        device_id_type=pl.DeviceIdType.MESH,
    )


def receipt(source, target, other, capacity, n_tile, send_sem, recv_sem):
    return pltpu.make_async_remote_copy(
        src_ref=source.at[pl.ds(other * capacity, capacity)],
        dst_ref=target.at[pl.ds(other * capacity, capacity)],
        send_sem=send_sem.at[other],
        recv_sem=recv_sem.at[other],
        device_id=address(other, n_tile),
        device_id_type=pl.DeviceIdType.MESH,
    )


def send_kernel(
    n_exp, n_tile, source, ident, weight, matched, warp_rows, warp_columns, route, slot, arrived,
    table, packed, send_sem, recv_sem,
):
    devices = n_exp * n_tile
    capacity = packed.shape[0] // devices
    me = lax.axis_index("exp") * n_tile + lax.axis_index("tile")
    greet(me, devices, n_tile)
    scale = weight[lax.axis_index("exp"), lax.axis_index("tile")]

    def warp(other, target):
        for rank in range(capacity):
            spot = other * capacity + rank
            which = ident[other, rank]
            first = jnp.dot(
                warp_rows[which], matched[source[other, rank]], preferred_element_type=jnp.float32
            ).astype(jnp.bfloat16)
            second = lax.dot_general(
                first,
                warp_columns[which],
                (((1,), (1,)), ((), ())),
                preferred_element_type=jnp.float32,
            )
            target[spot] = (scale * second).astype(target.dtype)

    def step(at, carry):
        other, _ = partner(me, at, devices)
        warp(other, packed)
        transfer(packed, arrived, me, other, capacity, n_tile, send_sem, recv_sem).start()
        return carry

    lax.fori_loop(0, devices - 1, step, 0)
    warp(me, arrived)

    hit = route[...] == me
    table[...] = by_rank(hit, ranked(hit), slot[...], SLOT_ROWS * SLOT_COLS, table.shape)

    def finish(at, carry):
        _, other = partner(me, at, devices)
        receipt(packed, arrived, other, capacity, n_tile, send_sem, recv_sem).wait()
        return carry

    lax.fori_loop(0, devices - 1, finish, 0)


def return_kernel(
    n_exp, n_tile, ident, place, table, value, warp_rows, warp_columns, image, above, below,
    picked, returned, unwarped, send_sem, recv_sem, edge_send, edge_recv,
):
    devices = n_exp * n_tile
    capacity = picked.shape[0] // devices
    across = image.shape[1] // BLOCK
    me = lax.axis_index("exp") * n_tile + lax.axis_index("tile")
    greet(me, devices, n_tile)

    def pick(other):
        for rank in range(capacity):
            picked[other * capacity + rank] = value[table[other, rank]]

    def begin(at, carry):
        other, _ = partner(me, at, devices)
        pick(other)
        transfer(picked, returned, me, other, capacity, n_tile, send_sem, recv_sem).start()
        return carry

    lax.fori_loop(0, devices - 1, begin, 0)

    def unwarp(other, origin):
        for rank in range(capacity):
            spot = other * capacity + rank
            which = ident[other, rank]
            back = lax.dot_general(
                warp_rows[which],
                origin[spot],
                (((0,), (0,)), ((), ())),
                preferred_element_type=jnp.float32,
            ).astype(jnp.bfloat16)
            piece = jnp.dot(back, warp_columns[which], preferred_element_type=jnp.float32)
            unwarped[spot] = piece.astype(unwarped.dtype)

    pick(me)
    unwarp(me, picked)

    def finish(at, carry):
        _, other = partner(me, at, devices)
        receipt(picked, returned, other, capacity, n_tile, send_sem, recv_sem).wait()
        unwarp(other, returned)
        return carry

    lax.fori_loop(0, devices - 1, finish, 0)

    def gather(at, carry):
        left = pl.multiple_of(at * BLOCK, BLOCK)
        for block in range(image.shape[0] // BLOCK):
            image[block * BLOCK : (block + 1) * BLOCK, pl.ds(left, BLOCK)] = unwarped[
                place[0, block * across + at]
            ]
        return carry

    lax.fori_loop(0, across, gather, 0)
    start_edges(image, above, below, edge_send, edge_recv)
    finish_edges(image, above, below, edge_send, edge_recv)


def coadd_kernel(n_tile, table, weight, arrived, patch, value, sums, total):
    slots = SLOT_ROWS * SLOT_COLS
    capacity = arrived.shape[0] // table.shape[0]
    blank = jnp.zeros((BLOCK, BLOCK), jnp.float32)

    def clear(at, carry):
        sums[at] = blank
        total[at] = 0.0
        return carry

    lax.fori_loop(0, slots + 1, clear, 0, unroll=5)

    def add(at, carry):
        share = weight[lax.div(at, n_tile), lax.rem(at, n_tile)]
        for rank in range(capacity):
            slot = table[at, rank]
            sums[slot] = sums[slot] + arrived[at * capacity + rank].astype(jnp.float32)
            total[slot] = total[slot] + share
        return carry

    lax.fori_loop(0, table.shape[0], add, 0, unroll=2)

    def divide(at, carry):
        for column in range(SLOT_COLS):
            number = at * SLOT_COLS + column
            weights = jnp.maximum(jnp.full((1, BLOCK), total[number], jnp.float32), 1.0)
            mean = sums[number] * (1.0 / weights)
            patch[
                pl.ds(pl.multiple_of(at * BLOCK, BLOCK), BLOCK),
                column * BLOCK : (column + 1) * BLOCK,
            ] = mean
            value[number] = mean.astype(value.dtype)
        return carry

    lax.fori_loop(0, SLOT_ROWS, divide, 0)
    value[slots] = blank.astype(value.dtype)


def difference_kernel(
    coef, above, image, below, row_bands, bands, exposure, difference, padded, passes
):
    cols = image.shape[1]
    row_stage(coef, above, image, below, row_bands, padded, passes)

    def step(at, carry):
        start = pl.multiple_of(at * WIDE, WIDE)
        matched = column_chunk(passes, bands, start)
        spot = pl.ds(start, WIDE)
        difference[:, spot] = exposure[:, spot].astype(jnp.float32) - matched
        return carry

    lax.fori_loop(0, cols // WIDE, step, 0, unroll=2)


def scalars(count):
    return [pl.BlockSpec(memory_space=pltpu.SMEM)] * count


def vectors(count):
    return [pl.BlockSpec(memory_space=pltpu.VMEM)] * count


def shards(
    exposure, row_taps, column_taps, basis_coef, warp_rows, warp_columns, warp_id, route_device,
    route_slot, weight,
):
    n_exp = lax.axis_size("exp")
    n_tile = lax.axis_size("tile")
    devices = n_exp * n_tile
    rows, cols = exposure.shape[1:]
    bases = row_taps.shape[0]
    blocks = (rows // BLOCK) * (cols // BLOCK)
    capacity = max(2, (2 * blocks + devices - 1) // devices)
    slots = SLOT_ROWS * SLOT_COLS
    buffered = devices * capacity
    mine = exposure[0]
    route = route_device.reshape(devices, blocks)
    slot = route_slot.reshape(devices, blocks)

    def shape(*dims, dtype=jnp.bfloat16):
        return jax.ShapeDtypeStruct(dims, dtype)

    def params(units, **more):
        return pltpu.CompilerParams(vmem_limit_bytes=units * 1024 * 1024, **more)

    buffer = shape(buffered, BLOCK, BLOCK)
    buffer_units = (2 * buffered * BLOCK * BLOCK) // (1024 * 1024)
    bank_units = (4 * warp_rows.size) // (1024 * 1024)
    image_units = (2 * rows * cols) // (1024 * 1024)
    work_units = (bases + 2) * image_units
    slot_units = (4 * slots * BLOCK * BLOCK) // (1024 * 1024)
    spare = 6
    tables = shape(devices, capacity, dtype=jnp.int32)
    edge = shape(RIM, cols)
    pair = [pltpu.SemaphoreType.DMA((2,)), pltpu.SemaphoreType.DMA((2,))]
    semaphores = [pltpu.SemaphoreType.DMA((devices,)), pltpu.SemaphoreType.DMA((devices,))]
    work = [
        pltpu.VMEM((rows + 2 * RIM, cols), jnp.bfloat16),
        pltpu.VMEM((bases, rows, cols + 2 * BLOCK), jnp.bfloat16),
    ]

    above, below, row_bands, bands, source, ident, place = pl.pallas_call(
        prepare_kernel,
        out_shape=(
            edge, edge, shape(bases * BLOCK, BLOCK + 2 * RIM), shape(bases, 2 * WIDE, WIDE),
            tables, tables, shape(1, blocks, dtype=jnp.int32),
        ),
        in_specs=[pl.BlockSpec(memory_space=pl.ANY)] + vectors(4),
        out_specs=tuple(vectors(7)),
        scratch_shapes=pair,
        compiler_params=params(spare + 4, collective_id=2, has_side_effects=True),
    )(mine, row_taps, column_taps, route, warp_id.reshape(devices, blocks))
    matched = pl.pallas_call(
        match_kernel,
        out_shape=shape(blocks + 1, BLOCK, BLOCK),
        in_specs=scalars(1) + vectors(5),
        out_specs=pl.BlockSpec(memory_space=pltpu.VMEM),
        scratch_shapes=work,
        compiler_params=params(work_units + 2 * image_units + spare),
    )(basis_coef, above, mine, below, row_bands, bands)
    arrived, table = pl.pallas_call(
        functools.partial(send_kernel, n_exp, n_tile),
        out_shape=(buffer, tables),
        in_specs=scalars(3) + vectors(5),
        out_specs=tuple(vectors(2)),
        scratch_shapes=[pltpu.VMEM(buffer.shape, buffer.dtype)] + semaphores,
        compiler_params=params(
            2 * buffer_units + bank_units + image_units + spare, collective_id=0,
            has_side_effects=True,
        ),
    )(source, ident, weight, matched, warp_rows, warp_columns, route, slot)
    patch, value = pl.pallas_call(
        functools.partial(coadd_kernel, n_tile),
        out_shape=(
            shape(SLOT_ROWS * BLOCK, SLOT_COLS * BLOCK, dtype=jnp.float32),
            shape(slots + 1, BLOCK, BLOCK),
        ),
        in_specs=scalars(2) + vectors(1),
        out_specs=tuple(vectors(2)),
        scratch_shapes=[
            pltpu.VMEM((slots + 1, BLOCK, BLOCK), jnp.float32),
            pltpu.SMEM((slots + 1,), jnp.float32),
        ],
        compiler_params=params(buffer_units + 3 * slot_units + spare),
    )(table, weight, arrived)
    template, template_above, template_below = pl.pallas_call(
        functools.partial(return_kernel, n_exp, n_tile),
        out_shape=(shape(rows, cols), edge, edge),
        in_specs=scalars(3) + vectors(3),
        out_specs=tuple(vectors(3)),
        scratch_shapes=[pltpu.VMEM(buffer.shape, buffer.dtype)] * 3 + semaphores + pair,
        compiler_params=params(
            3 * buffer_units + bank_units + slot_units + image_units + spare, collective_id=1,
            has_side_effects=True,
        ),
    )(ident, place, table, value, warp_rows, warp_columns)
    difference = pl.pallas_call(
        difference_kernel,
        out_shape=shape(rows, cols, dtype=jnp.float32),
        in_specs=scalars(1) + vectors(6),
        out_specs=pl.BlockSpec(memory_space=pltpu.VMEM),
        scratch_shapes=work,
        compiler_params=params(work_units + 4 * image_units + spare),
    )(basis_coef, template_above, template, template_below, row_bands, bands, mine)
    return patch, difference[None]


def solution(mesh):
    placed = (P("exp", "tile", None), P(), P(), P("exp", None), P(), P(), P(), P(), P(), P())
    return jax.shard_map(
        shards,
        mesh=mesh,
        in_specs=placed,
        out_specs=(P("exp", "tile"), P("exp", "tile", None)),
        check_vma=False,
    )
```

```python
import functools

import jax
import jax.numpy as jnp
from jax import lax
from jax.experimental import pallas as pl
from jax.experimental.pallas import tpu as pltpu
from jax.sharding import PartitionSpec as P

BLOCK = 128
HALF = 10
RIM = 16
WIDE = 2 * BLOCK
SLOT_ROWS = 8
SLOT_COLS = 8


def edge_copies(image, above, below, send_sem, recv_sem):
    rows = image.shape[0]
    row, tile, count = lax.axis_index("exp"), lax.axis_index("tile"), lax.axis_size("tile")
    onward = pltpu.make_async_remote_copy(
        src_ref=image.at[pl.ds(rows - RIM, RIM)],
        dst_ref=above,
        send_sem=send_sem.at[0],
        recv_sem=recv_sem.at[0],
        device_id=(row, lax.rem(tile + 1, count)),
        device_id_type=pl.DeviceIdType.MESH,
    )
    backward = pltpu.make_async_remote_copy(
        src_ref=image.at[pl.ds(0, RIM)],
        dst_ref=below,
        send_sem=send_sem.at[1],
        recv_sem=recv_sem.at[1],
        device_id=(row, lax.rem(tile + count - 1, count)),
        device_id_type=pl.DeviceIdType.MESH,
    )
    return onward, backward


def start_edges(image, above, below, send_sem, recv_sem):
    tile, count = lax.axis_index("tile"), lax.axis_size("tile")
    onward, backward = edge_copies(image, above, below, send_sem, recv_sem)

    @pl.when(tile < count - 1)
    def _():
        onward.start()

    @pl.when(tile > 0)
    def _():
        backward.start()

    @pl.when(tile == 0)
    def _():
        above[...] = jnp.zeros_like(above)

    @pl.when(tile == count - 1)
    def _():
        below[...] = jnp.zeros_like(below)


def finish_edges(image, above, below, send_sem, recv_sem):
    tile, count = lax.axis_index("tile"), lax.axis_size("tile")
    onward, backward = edge_copies(image, above, below, send_sem, recv_sem)

    @pl.when(tile < count - 1)
    def _():
        onward.wait_send()
        backward.wait_recv()

    @pl.when(tile > 0)
    def _():
        backward.wait_send()
        onward.wait_recv()


def banded(taps, basis, lag):
    total = jnp.zeros(lag.shape, jnp.float32)
    for tap in range(taps.shape[1]):
        value = jnp.broadcast_to(taps[basis : basis + 1, tap : tap + 1], lag.shape)
        total = jnp.where(lag == tap, value, total)
    return total.astype(jnp.bfloat16)


def ranked(hit):
    count = hit.shape[1]
    later = (
        lax.broadcasted_iota(jnp.int32, (count, count), 0)
        < lax.broadcasted_iota(jnp.int32, (count, count), 1)
    )
    ranks = jnp.dot(
        hit.astype(jnp.float32), later.astype(jnp.float32), preferred_element_type=jnp.float32
    )
    return ranks.astype(jnp.int32)


def by_rank(hit, ranks, values, none, shape):
    column = lax.broadcasted_iota(jnp.int32, shape, 1)
    filled = jnp.zeros(shape, jnp.int32)
    for rank in range(shape[1]):
        chosen = jnp.where(hit & (ranks == rank), values - none, 0)
        filled = jnp.where(column == rank, jnp.sum(chosen, axis=1, keepdims=True) + none, filled)
    return filled


def prepare_kernel(
    image, row_taps, column_taps, route_all, warp_all, above, below, row_bands, bands, source,
    ident, place, send_sem, recv_sem, route, warp_id, load_sem,
):
    row, tile, count = lax.axis_index("exp"), lax.axis_index("tile"), lax.axis_size("tile")
    me = row * count + tile
    load_route = pltpu.make_async_copy(route_all, route, load_sem.at[0])
    load_warp = pltpu.make_async_copy(warp_all, warp_id, load_sem.at[1])
    load_route.start()
    load_warp.start()
    barrier = pltpu.get_barrier_semaphore()

    @pl.when(tile < count - 1)
    def _():
        pl.semaphore_signal(
            barrier, inc=1, device_id=(row, lax.rem(tile + 1, count)),
            device_id_type=pl.DeviceIdType.MESH,
        )

    @pl.when(tile > 0)
    def _():
        pl.semaphore_signal(
            barrier, inc=1, device_id=(row, lax.rem(tile + count - 1, count)),
            device_id_type=pl.DeviceIdType.MESH,
        )

    bases = row_taps.shape[0]
    taps = row_taps[...].astype(jnp.float32)
    shape = (BLOCK, BLOCK + 2 * RIM)
    lag = lax.broadcasted_iota(jnp.int32, shape, 1) - lax.broadcasted_iota(jnp.int32, shape, 0)
    for basis in range(bases):
        row_bands[basis * BLOCK : (basis + 1) * BLOCK, :] = banded(
            taps, basis, lag - (RIM - HALF)
        )

    peers = jnp.minimum(tile, 1) + jnp.minimum(count - 1 - tile, 1)
    pl.semaphore_wait(barrier, peers)

    start_edges(image, above, below, send_sem, recv_sem)

    taps = column_taps[...].astype(jnp.float32)
    shape = (3 * BLOCK, BLOCK)
    lag = lax.broadcasted_iota(jnp.int32, shape, 0) - lax.broadcasted_iota(jnp.int32, shape, 1)
    bands[...] = jnp.zeros_like(bands)
    for basis in range(bases):
        band = banded(taps, basis, lag - (BLOCK - HALF))
        for side in range(WIDE // BLOCK):
            top = side * BLOCK
            bands[basis, top : top + 3 * BLOCK, top : top + BLOCK] = band

    load_route.wait()
    load_warp.wait()
    devices, blocks = route.shape
    capacity = source.shape[1]
    device = lax.broadcasted_iota(jnp.int32, (devices, blocks), 0)
    hit = jnp.broadcast_to(route[pl.ds(me, 1), :], (devices, blocks)) == device
    ranks = ranked(hit)
    number = lax.broadcasted_iota(jnp.int32, (devices, blocks), 1)
    source[...] = by_rank(hit, ranks, number, blocks, source.shape)
    mine = jnp.broadcast_to(warp_id[pl.ds(me, 1), :], (devices, blocks))
    ident[...] = by_rank(hit, ranks, mine, 0, ident.shape)
    place[...] = jnp.sum(jnp.where(hit, device * capacity + ranks, 0), axis=0, keepdims=True)

    finish_edges(image, above, below, send_sem, recv_sem)


def row_stage(coef, above, image, below, row_bands, padded, passes):
    bases = passes.shape[0]
    rows, cols = image.shape
    blocks = rows // BLOCK
    span = BLOCK + 2 * RIM
    padded[:RIM, :] = above[...]
    padded[RIM : RIM + rows, :] = image[...]
    padded[RIM + rows :, :] = below[...]
    edge = jnp.zeros((rows, BLOCK), passes.dtype)
    for basis in range(bases):
        passes[basis, :, :BLOCK] = edge
        passes[basis, :, BLOCK + cols :] = edge

    def step(at, carry):
        start = pl.multiple_of(at * WIDE, WIDE)
        for block in range(blocks):
            top = block * BLOCK
            sums = jnp.dot(
                row_bands[...],
                padded[top : top + span, pl.ds(start, WIDE)],
                preferred_element_type=jnp.float32,
            )
            for basis in range(bases):
                scaled = coef[0, basis] * sums[basis * BLOCK : (basis + 1) * BLOCK]
                passes[basis, top : top + BLOCK, pl.ds(start + BLOCK, WIDE)] = scaled.astype(
                    passes.dtype
                )
        return carry

    lax.fori_loop(0, cols // WIDE, step, 0, unroll=2)


def column_chunk(passes, column_bands, start):
    total = None
    for basis in range(passes.shape[0]):
        term = jnp.dot(
            passes[basis, :, pl.ds(start, 2 * WIDE)],
            column_bands[basis],
            preferred_element_type=jnp.float32,
        )
        total = term if total is None else total + term
    return total


def match_kernel(coef, above, image, below, row_bands, bands, matched, padded, passes):
    rows, cols = image.shape
    blocks = rows // BLOCK
    across = cols // BLOCK
    row_stage(coef, above, image, below, row_bands, padded, passes)
    matched[blocks * across] = jnp.zeros((BLOCK, BLOCK), matched.dtype)

    def step(at, carry):
        start = pl.multiple_of(at * WIDE, WIDE)
        chunk = column_chunk(passes, bands, start).astype(matched.dtype)
        for block in range(blocks):
            for side in range(WIDE // BLOCK):
                number = block * across + at * (WIDE // BLOCK) + side
                matched[number] = chunk[
                    block * BLOCK : (block + 1) * BLOCK, side * BLOCK : (side + 1) * BLOCK
                ]
        return carry

    lax.fori_loop(0, cols // WIDE, step, 0, unroll=2)


def partner(me, step, devices):
    half = devices // 2
    pair = lax.div(step, 2)
    odd = lax.rem(pair, 2)
    far = half + (2 * odd - 1) * lax.div(pair + 1, 2)
    near = (1 - odd) * (1 + lax.div(pair, 2)) + odd * (devices - 1 - lax.div(pair, 2))
    turn = lax.rem(step, 2)
    shift = (1 - turn) * far + turn * near
    return lax.rem(me + shift, devices), lax.rem(me + devices - shift, devices)


def address(device, n_tile):
    return (lax.div(device, n_tile), lax.rem(device, n_tile))


def greet(me, devices, n_tile):
    barrier = pltpu.get_barrier_semaphore()

    def hello(step, carry):
        other = lax.rem(me + step + 1, devices)
        pl.semaphore_signal(
            barrier, inc=1, device_id=address(other, n_tile), device_id_type=pl.DeviceIdType.MESH
        )
        return carry

    lax.fori_loop(0, devices - 1, hello, 0)
    return barrier


def transfer(source, target, me, other, capacity, n_tile, send_sem, recv_sem):
    for rank in range(capacity):
        pltpu.make_async_remote_copy(
            src_ref=source.at[pl.ds(other * capacity + rank, 1)],
            dst_ref=target.at[pl.ds(me * capacity + rank, 1)],
            send_sem=send_sem.at[other],
            recv_sem=recv_sem.at[me],
            device_id=address(other, n_tile),
            device_id_type=pl.DeviceIdType.MESH,
        ).start()


def receipt(source, target, other, capacity, n_tile, send_sem, recv_sem):
    return pltpu.make_async_remote_copy(
        src_ref=source.at[pl.ds(other * capacity, capacity)],
        dst_ref=target.at[pl.ds(other * capacity, capacity)],
        send_sem=send_sem.at[other],
        recv_sem=recv_sem.at[other],
        device_id=address(other, n_tile),
        device_id_type=pl.DeviceIdType.MESH,
    )


def send_kernel(
    n_exp, n_tile, source, ident, weight, matched, warp_rows, warp_columns, route, slot, arrived,
    table, packed, send_sem, recv_sem,
):
    devices = n_exp * n_tile
    capacity = packed.shape[0] // devices
    me = lax.axis_index("exp") * n_tile + lax.axis_index("tile")
    barrier = greet(me, devices, n_tile)
    scale = weight[lax.axis_index("exp"), lax.axis_index("tile")]

    def warp(other, target):
        for rank in range(capacity):
            spot = other * capacity + rank
            which = ident[other, rank]
            first = jnp.dot(
                warp_rows[which], matched[source[other, rank]], preferred_element_type=jnp.float32
            ).astype(jnp.bfloat16)
            second = lax.dot_general(
                first,
                warp_columns[which],
                (((1,), (1,)), ((), ())),
                preferred_element_type=jnp.float32,
            )
            target[spot] = (scale * second).astype(target.dtype)

    warp(me, arrived)
    pl.semaphore_wait(barrier, devices - 1)

    def step(at, carry):
        other, _ = partner(me, at, devices)
        warp(other, packed)
        transfer(packed, arrived, me, other, capacity, n_tile, send_sem, recv_sem)
        return carry

    lax.fori_loop(0, devices - 1, step, 0)

    hit = route[...] == me
    table[...] = by_rank(hit, ranked(hit), slot[...], SLOT_ROWS * SLOT_COLS, table.shape)

    def finish(at, carry):
        _, other = partner(me, at, devices)
        receipt(packed, arrived, other, capacity, n_tile, send_sem, recv_sem).wait()
        return carry

    lax.fori_loop(0, devices - 1, finish, 0)


def return_kernel(
    n_exp, n_tile, ident, place, table, value, warp_rows, warp_columns, image, above, below,
    picked, returned, unwarped, send_sem, recv_sem, edge_send, edge_recv,
):
    devices = n_exp * n_tile
    capacity = picked.shape[0] // devices
    across = image.shape[1] // BLOCK
    me = lax.axis_index("exp") * n_tile + lax.axis_index("tile")
    barrier = greet(me, devices, n_tile)

    def pick(other):
        for rank in range(capacity):
            picked[other * capacity + rank] = value[table[other, rank]]

    pick(me)
    pl.semaphore_wait(barrier, devices - 1)

    def begin(at, carry):
        other, _ = partner(me, at, devices)
        pick(other)
        transfer(picked, returned, me, other, capacity, n_tile, send_sem, recv_sem)
        return carry

    lax.fori_loop(0, devices - 1, begin, 0)

    def unwarp(other, origin):
        for rank in range(capacity):
            spot = other * capacity + rank
            which = ident[other, rank]
            back = lax.dot_general(
                warp_rows[which],
                origin[spot],
                (((0,), (0,)), ((), ())),
                preferred_element_type=jnp.float32,
            ).astype(jnp.bfloat16)
            piece = jnp.dot(back, warp_columns[which], preferred_element_type=jnp.float32)
            unwarped[spot] = piece.astype(unwarped.dtype)

    unwarp(me, picked)

    def finish(at, carry):
        _, other = partner(me, at, devices)
        receipt(picked, returned, other, capacity, n_tile, send_sem, recv_sem).wait()
        unwarp(other, returned)
        return carry

    lax.fori_loop(0, devices - 1, finish, 0)

    def gather(at, carry):
        left = pl.multiple_of(at * BLOCK, BLOCK)
        for block in range(image.shape[0] // BLOCK):
            image[block * BLOCK : (block + 1) * BLOCK, pl.ds(left, BLOCK)] = unwarped[
                place[0, block * across + at]
            ]
        return carry

    lax.fori_loop(0, across, gather, 0)
    start_edges(image, above, below, edge_send, edge_recv)
    finish_edges(image, above, below, edge_send, edge_recv)


def coadd_kernel(n_tile, table, weight, arrived, patch_out, value, sums, total, patch, done):
    slots = SLOT_ROWS * SLOT_COLS
    capacity = arrived.shape[0] // table.shape[0]
    blank = jnp.zeros((BLOCK, BLOCK), jnp.float32)

    def clear(at, carry):
        sums[at] = blank
        total[at] = 0.0
        return carry

    lax.fori_loop(0, slots + 1, clear, 0, unroll=5)

    def add(at, carry):
        share = weight[lax.div(at, n_tile), lax.rem(at, n_tile)]
        for rank in range(capacity):
            slot = table[at, rank]
            sums[slot] = sums[slot] + arrived[at * capacity + rank].astype(jnp.float32)
            total[slot] = total[slot] + share
        return carry

    lax.fori_loop(0, table.shape[0], add, 0, unroll=2)

    def divide(at, carry):
        for column in range(SLOT_COLS):
            number = at * SLOT_COLS + column
            weights = jnp.maximum(jnp.full((1, BLOCK), total[number], jnp.float32), 1.0)
            mean = sums[number] * (1.0 / weights)
            patch[
                pl.ds(pl.multiple_of(at * BLOCK, BLOCK), BLOCK),
                column * BLOCK : (column + 1) * BLOCK,
            ] = mean
            value[number] = mean.astype(value.dtype)
        strip = pl.ds(pl.multiple_of(at * BLOCK, BLOCK), BLOCK)
        pltpu.make_async_copy(patch.at[strip], patch_out.at[strip], done).start()
        return carry

    lax.fori_loop(0, SLOT_ROWS, divide, 0)
    value[slots] = blank.astype(value.dtype)
    pltpu.make_async_copy(patch, patch_out, done).wait()


def difference_kernel(
    coef, above, image, below, row_bands, bands, exposure, difference_out, padded, passes,
    difference, done,
):
    cols = image.shape[1]
    row_stage(coef, above, image, below, row_bands, padded, passes)

    def step(at, carry):
        start = pl.multiple_of(at * WIDE, WIDE)
        matched = column_chunk(passes, bands, start)
        spot = pl.ds(start, WIDE)
        difference[:, spot] = exposure[:, spot].astype(jnp.float32) - matched
        pltpu.make_async_copy(difference.at[:, spot], difference_out.at[:, spot], done).start()
        return carry

    lax.fori_loop(0, cols // WIDE, step, 0, unroll=2)
    pltpu.make_async_copy(difference, difference_out, done).wait()


def scalars(count):
    return [pl.BlockSpec(memory_space=pltpu.SMEM)] * count


def vectors(count):
    return [pl.BlockSpec(memory_space=pltpu.VMEM)] * count


def far(count):
    return [pl.BlockSpec(memory_space=pltpu.HBM)] * count


def shards(
    exposure, row_taps, column_taps, basis_coef, warp_rows, warp_columns, warp_id, route_device,
    route_slot, weight,
):
    n_exp = lax.axis_size("exp")
    n_tile = lax.axis_size("tile")
    devices = n_exp * n_tile
    rows, cols = exposure.shape[1:]
    bases = row_taps.shape[0]
    blocks = (rows // BLOCK) * (cols // BLOCK)
    capacity = max(2, (2 * blocks + devices - 1) // devices)
    slots = SLOT_ROWS * SLOT_COLS
    buffered = devices * capacity
    mine = exposure[0]
    route = route_device.reshape(devices, blocks)
    slot = route_slot.reshape(devices, blocks)

    def shape(*dims, dtype=jnp.bfloat16):
        return jax.ShapeDtypeStruct(dims, dtype)

    def params(units, **more):
        return pltpu.CompilerParams(vmem_limit_bytes=units * 1024 * 1024, **more)

    buffer = shape(buffered, BLOCK, BLOCK)
    buffer_units = (2 * buffered * BLOCK * BLOCK) // (1024 * 1024)
    bank_units = (4 * warp_rows.size) // (1024 * 1024)
    image_units = (2 * rows * cols) // (1024 * 1024)
    work_units = (bases + 2) * image_units
    slot_units = (4 * slots * BLOCK * BLOCK) // (1024 * 1024)
    spare = 6
    tables = shape(devices, capacity, dtype=jnp.int32)
    edge = shape(RIM, cols)
    pair = [pltpu.SemaphoreType.DMA((2,)), pltpu.SemaphoreType.DMA((2,))]
    semaphores = [pltpu.SemaphoreType.DMA((devices,)), pltpu.SemaphoreType.DMA((devices,))]
    work = [
        pltpu.VMEM((rows + 2 * RIM, cols), jnp.bfloat16),
        pltpu.VMEM((bases, rows, cols + 2 * BLOCK), jnp.bfloat16),
    ]

    above, below, row_bands, bands, source, ident, place = pl.pallas_call(
        prepare_kernel,
        out_shape=(
            edge, edge, shape(bases * BLOCK, BLOCK + 2 * RIM), shape(bases, 2 * WIDE, WIDE),
            tables, tables, shape(1, blocks, dtype=jnp.int32),
        ),
        in_specs=far(1) + vectors(2) + far(2),
        out_specs=tuple(vectors(7)),
        scratch_shapes=pair + [
            pltpu.VMEM((devices, blocks), jnp.int32),
            pltpu.VMEM((devices, blocks), jnp.int32),
            pltpu.SemaphoreType.DMA((2,)),
        ],
        compiler_params=params(spare + 4, collective_id=2, has_side_effects=True),
    )(mine, row_taps, column_taps, route, warp_id.reshape(devices, blocks))
    matched = pl.pallas_call(
        match_kernel,
        out_shape=shape(blocks + 1, BLOCK, BLOCK),
        in_specs=scalars(1) + vectors(5),
        out_specs=pl.BlockSpec(memory_space=pltpu.VMEM),
        scratch_shapes=work,
        compiler_params=params(work_units + 2 * image_units + spare),
    )(basis_coef, above, mine, below, row_bands, bands)
    arrived, table = pl.pallas_call(
        functools.partial(send_kernel, n_exp, n_tile),
        out_shape=(buffer, tables),
        in_specs=scalars(3) + vectors(5),
        out_specs=tuple(vectors(2)),
        scratch_shapes=[pltpu.VMEM(buffer.shape, buffer.dtype)] + semaphores,
        compiler_params=params(
            2 * buffer_units + bank_units + image_units + spare, collective_id=0,
            has_side_effects=True,
        ),
    )(source, ident, weight, matched, warp_rows, warp_columns, route, slot)
    patch, value = pl.pallas_call(
        functools.partial(coadd_kernel, n_tile),
        out_shape=(
            shape(SLOT_ROWS * BLOCK, SLOT_COLS * BLOCK, dtype=jnp.float32),
            shape(slots + 1, BLOCK, BLOCK),
        ),
        in_specs=scalars(2) + vectors(1),
        out_specs=tuple(far(1) + vectors(1)),
        scratch_shapes=[
            pltpu.VMEM((slots + 1, BLOCK, BLOCK), jnp.float32),
            pltpu.SMEM((slots + 1,), jnp.float32),
            pltpu.VMEM((SLOT_ROWS * BLOCK, SLOT_COLS * BLOCK), jnp.float32),
            pltpu.SemaphoreType.DMA(()),
        ],
        compiler_params=params(buffer_units + 3 * slot_units + spare),
    )(table, weight, arrived)
    template, template_above, template_below = pl.pallas_call(
        functools.partial(return_kernel, n_exp, n_tile),
        out_shape=(shape(rows, cols), edge, edge),
        in_specs=scalars(3) + vectors(3),
        out_specs=tuple(vectors(3)),
        scratch_shapes=[pltpu.VMEM(buffer.shape, buffer.dtype)] * 3 + semaphores + pair,
        compiler_params=params(
            3 * buffer_units + bank_units + slot_units + image_units + spare, collective_id=1,
            has_side_effects=True,
        ),
    )(ident, place, table, value, warp_rows, warp_columns)
    difference = pl.pallas_call(
        difference_kernel,
        out_shape=shape(rows, cols, dtype=jnp.float32),
        in_specs=scalars(1) + vectors(6),
        out_specs=far(1)[0],
        scratch_shapes=work + [
            pltpu.VMEM((rows, cols), jnp.float32), pltpu.SemaphoreType.DMA(()),
        ],
        compiler_params=params(work_units + 4 * image_units + spare),
    )(basis_coef, template_above, template, template_below, row_bands, bands, mine)
    return patch, difference[None]


def solution(mesh):
    placed = (P("exp", "tile", None), P(), P(), P("exp", None), P(), P(), P(), P(), P(), P())
    return jax.shard_map(
        shards,
        mesh=mesh,
        in_specs=placed,
        out_specs=(P("exp", "tile"), P("exp", "tile", None)),
        check_vma=False,
    )
```

```python
import functools

import jax
import jax.numpy as jnp
from jax import lax
from jax.experimental import pallas as pl
from jax.experimental.pallas import tpu as pltpu
from jax.sharding import PartitionSpec as P

BLOCK = 128
HALF = 10
RIM = 16
WIDE = 2 * BLOCK
SLOT_ROWS = 8
SLOT_COLS = 8


def edge_copies(image, above, below, send_sem, recv_sem):
    rows = image.shape[0]
    row, tile, count = lax.axis_index("exp"), lax.axis_index("tile"), lax.axis_size("tile")
    onward = pltpu.make_async_remote_copy(
        src_ref=image.at[pl.ds(rows - RIM, RIM)],
        dst_ref=above,
        send_sem=send_sem.at[0],
        recv_sem=recv_sem.at[0],
        device_id=(row, lax.rem(tile + 1, count)),
        device_id_type=pl.DeviceIdType.MESH,
    )
    backward = pltpu.make_async_remote_copy(
        src_ref=image.at[pl.ds(0, RIM)],
        dst_ref=below,
        send_sem=send_sem.at[1],
        recv_sem=recv_sem.at[1],
        device_id=(row, lax.rem(tile + count - 1, count)),
        device_id_type=pl.DeviceIdType.MESH,
    )
    return onward, backward


def start_edges(image, above, below, send_sem, recv_sem):
    tile, count = lax.axis_index("tile"), lax.axis_size("tile")
    onward, backward = edge_copies(image, above, below, send_sem, recv_sem)

    @pl.when(tile < count - 1)
    def _():
        onward.start()

    @pl.when(tile > 0)
    def _():
        backward.start()

    @pl.when(tile == 0)
    def _():
        above[...] = jnp.zeros_like(above)

    @pl.when(tile == count - 1)
    def _():
        below[...] = jnp.zeros_like(below)


def finish_edges(image, above, below, send_sem, recv_sem):
    tile, count = lax.axis_index("tile"), lax.axis_size("tile")
    onward, backward = edge_copies(image, above, below, send_sem, recv_sem)

    @pl.when(tile < count - 1)
    def _():
        onward.wait_send()
        backward.wait_recv()

    @pl.when(tile > 0)
    def _():
        backward.wait_send()
        onward.wait_recv()


def banded(taps, basis, lag):
    total = jnp.zeros(lag.shape, jnp.float32)
    for tap in range(taps.shape[1]):
        value = jnp.broadcast_to(taps[basis : basis + 1, tap : tap + 1], lag.shape)
        total = jnp.where(lag == tap, value, total)
    return total.astype(jnp.bfloat16)


def ranked(hit):
    count = hit.shape[1]
    later = (
        lax.broadcasted_iota(jnp.int32, (count, count), 0)
        < lax.broadcasted_iota(jnp.int32, (count, count), 1)
    )
    ranks = jnp.dot(
        hit.astype(jnp.float32), later.astype(jnp.float32), preferred_element_type=jnp.float32
    )
    return ranks.astype(jnp.int32)


def by_rank(hit, ranks, values, none, shape):
    column = lax.broadcasted_iota(jnp.int32, shape, 1)
    filled = jnp.zeros(shape, jnp.int32)
    for rank in range(shape[1]):
        chosen = jnp.where(hit & (ranks == rank), values - none, 0)
        filled = jnp.where(column == rank, jnp.sum(chosen, axis=1, keepdims=True) + none, filled)
    return filled


def prepare_kernel(
    image, row_taps, column_taps, route_all, warp_all, above, below, row_bands, bands, source,
    ident, place, send_sem, recv_sem, route, warp_id, load_sem,
):
    row, tile, count = lax.axis_index("exp"), lax.axis_index("tile"), lax.axis_size("tile")
    me = row * count + tile
    load_route = pltpu.make_async_copy(route_all, route, load_sem.at[0])
    load_warp = pltpu.make_async_copy(warp_all, warp_id, load_sem.at[1])
    load_route.start()
    load_warp.start()
    barrier = pltpu.get_barrier_semaphore()

    @pl.when(tile < count - 1)
    def _():
        pl.semaphore_signal(
            barrier, inc=1, device_id=(row, lax.rem(tile + 1, count)),
            device_id_type=pl.DeviceIdType.MESH,
        )

    @pl.when(tile > 0)
    def _():
        pl.semaphore_signal(
            barrier, inc=1, device_id=(row, lax.rem(tile + count - 1, count)),
            device_id_type=pl.DeviceIdType.MESH,
        )

    bases = row_taps.shape[0]
    taps = row_taps[...].astype(jnp.float32)
    shape = (BLOCK, BLOCK + 2 * RIM)
    lag = lax.broadcasted_iota(jnp.int32, shape, 1) - lax.broadcasted_iota(jnp.int32, shape, 0)
    for basis in range(bases):
        row_bands[basis * BLOCK : (basis + 1) * BLOCK, :] = banded(
            taps, basis, lag - (RIM - HALF)
        )

    peers = jnp.minimum(tile, 1) + jnp.minimum(count - 1 - tile, 1)
    pl.semaphore_wait(barrier, peers)

    start_edges(image, above, below, send_sem, recv_sem)

    taps = column_taps[...].astype(jnp.float32)
    shape = (3 * BLOCK, BLOCK)
    lag = lax.broadcasted_iota(jnp.int32, shape, 0) - lax.broadcasted_iota(jnp.int32, shape, 1)
    bands[...] = jnp.zeros_like(bands)
    for basis in range(bases):
        band = banded(taps, basis, lag - (BLOCK - HALF))
        for side in range(WIDE // BLOCK):
            top = side * BLOCK
            bands[basis, top : top + 3 * BLOCK, top : top + BLOCK] = band

    load_route.wait()
    load_warp.wait()
    devices, blocks = route.shape
    capacity = source.shape[1]
    device = lax.broadcasted_iota(jnp.int32, (devices, blocks), 0)
    hit = jnp.broadcast_to(route[pl.ds(me, 1), :], (devices, blocks)) == device
    ranks = ranked(hit)
    number = lax.broadcasted_iota(jnp.int32, (devices, blocks), 1)
    source[...] = by_rank(hit, ranks, number, blocks, source.shape)
    mine = jnp.broadcast_to(warp_id[pl.ds(me, 1), :], (devices, blocks))
    ident[...] = by_rank(hit, ranks, mine, 0, ident.shape)
    place[...] = jnp.sum(jnp.where(hit, device * capacity + ranks, 0), axis=0, keepdims=True)

    finish_edges(image, above, below, send_sem, recv_sem)


def row_stage(coef, above, image, below, row_bands, padded, passes):
    bases = passes.shape[0]
    rows, cols = image.shape
    blocks = rows // BLOCK
    span = BLOCK + 2 * RIM
    padded[:RIM, :] = above[...]
    padded[RIM : RIM + rows, :] = image[...]
    padded[RIM + rows :, :] = below[...]
    edge = jnp.zeros((rows, BLOCK), passes.dtype)
    for basis in range(bases):
        passes[basis, :, :BLOCK] = edge
        passes[basis, :, BLOCK + cols :] = edge

    def step(at, carry):
        start = pl.multiple_of(at * WIDE, WIDE)
        for block in range(blocks):
            top = block * BLOCK
            sums = jnp.dot(
                row_bands[...],
                padded[top : top + span, pl.ds(start, WIDE)],
                preferred_element_type=jnp.float32,
            )
            for basis in range(bases):
                scaled = coef[0, basis] * sums[basis * BLOCK : (basis + 1) * BLOCK]
                passes[basis, top : top + BLOCK, pl.ds(start + BLOCK, WIDE)] = scaled.astype(
                    passes.dtype
                )
        return carry

    lax.fori_loop(0, cols // WIDE, step, 0, unroll=2)


def column_chunk(passes, column_bands, start):
    total = None
    for basis in range(passes.shape[0]):
        term = jnp.dot(
            passes[basis, :, pl.ds(start, 2 * WIDE)],
            column_bands[basis],
            preferred_element_type=jnp.float32,
        )
        total = term if total is None else total + term
    return total


def match_kernel(coef, above, image, below, row_bands, bands, matched, padded, passes):
    rows, cols = image.shape
    blocks = rows // BLOCK
    across = cols // BLOCK
    row_stage(coef, above, image, below, row_bands, padded, passes)
    matched[blocks * across] = jnp.zeros((BLOCK, BLOCK), matched.dtype)

    def step(at, carry):
        start = pl.multiple_of(at * WIDE, WIDE)
        chunk = column_chunk(passes, bands, start).astype(matched.dtype)
        for block in range(blocks):
            for side in range(WIDE // BLOCK):
                number = block * across + at * (WIDE // BLOCK) + side
                matched[number] = chunk[
                    block * BLOCK : (block + 1) * BLOCK, side * BLOCK : (side + 1) * BLOCK
                ]
        return carry

    lax.fori_loop(0, cols // WIDE, step, 0, unroll=2)


def partner(me, step, n_exp, n_tile):
    row, tile = lax.div(me, n_tile), lax.rem(me, n_tile)
    down = lax.rem(step, n_exp)
    across = lax.rem(lax.div(step, n_exp) + 2 * down, n_tile)
    target = lax.rem(row + down, n_exp) * n_tile + lax.rem(tile + across, n_tile)
    origin = lax.rem(row + n_exp - down, n_exp) * n_tile + lax.rem(tile + n_tile - across, n_tile)
    return target, origin


def address(device, n_tile):
    return (lax.div(device, n_tile), lax.rem(device, n_tile))


def greet(me, devices, n_tile):
    barrier = pltpu.get_barrier_semaphore()

    def hello(step, carry):
        other = lax.rem(me + step + 1, devices)
        pl.semaphore_signal(
            barrier, inc=1, device_id=address(other, n_tile), device_id_type=pl.DeviceIdType.MESH
        )
        return carry

    lax.fori_loop(0, devices - 1, hello, 0)
    return barrier


def transfer(source, target, me, other, capacity, n_tile, send_sem, recv_sem):
    for rank in range(capacity):
        pltpu.make_async_remote_copy(
            src_ref=source.at[pl.ds(other * capacity + rank, 1)],
            dst_ref=target.at[pl.ds(me * capacity + rank, 1)],
            send_sem=send_sem.at[other],
            recv_sem=recv_sem.at[me],
            device_id=address(other, n_tile),
            device_id_type=pl.DeviceIdType.MESH,
        ).start()


def receipt(source, target, other, capacity, n_tile, send_sem, recv_sem):
    return pltpu.make_async_remote_copy(
        src_ref=source.at[pl.ds(other * capacity, capacity)],
        dst_ref=target.at[pl.ds(other * capacity, capacity)],
        send_sem=send_sem.at[other],
        recv_sem=recv_sem.at[other],
        device_id=address(other, n_tile),
        device_id_type=pl.DeviceIdType.MESH,
    )


def send_kernel(
    n_exp, n_tile, source, ident, weight, matched, warp_rows, warp_columns, route, slot, arrived,
    table, packed, send_sem, recv_sem,
):
    devices = n_exp * n_tile
    capacity = packed.shape[0] // devices
    me = lax.axis_index("exp") * n_tile + lax.axis_index("tile")
    barrier = greet(me, devices, n_tile)
    scale = weight[lax.axis_index("exp"), lax.axis_index("tile")]

    def warp(other, target):
        for rank in range(capacity):
            spot = other * capacity + rank
            which = ident[other, rank]
            first = jnp.dot(
                warp_rows[which], matched[source[other, rank]], preferred_element_type=jnp.float32
            ).astype(jnp.bfloat16)
            second = lax.dot_general(
                first,
                warp_columns[which],
                (((1,), (1,)), ((), ())),
                preferred_element_type=jnp.float32,
            )
            target[spot] = (scale * second).astype(target.dtype)

    warp(me, arrived)
    pl.semaphore_wait(barrier, devices - 1)

    def step(at, carry):
        other, _ = partner(me, at, n_exp, n_tile)
        warp(other, packed)
        transfer(packed, arrived, me, other, capacity, n_tile, send_sem, recv_sem)
        return carry

    lax.fori_loop(1, devices, step, 0)

    hit = route[...] == me
    table[...] = by_rank(hit, ranked(hit), slot[...], SLOT_ROWS * SLOT_COLS, table.shape)

    def finish(at, carry):
        _, other = partner(me, at, n_exp, n_tile)
        receipt(packed, arrived, other, capacity, n_tile, send_sem, recv_sem).wait()
        return carry

    lax.fori_loop(1, devices, finish, 0)


def return_kernel(
    n_exp, n_tile, ident, place, table, value, warp_rows, warp_columns, image, above, below,
    picked, returned, unwarped, send_sem, recv_sem, edge_send, edge_recv,
):
    devices = n_exp * n_tile
    capacity = picked.shape[0] // devices
    across = image.shape[1] // BLOCK
    me = lax.axis_index("exp") * n_tile + lax.axis_index("tile")
    barrier = greet(me, devices, n_tile)

    def pick(other):
        for rank in range(capacity):
            picked[other * capacity + rank] = value[table[other, rank]]

    pick(me)
    pl.semaphore_wait(barrier, devices - 1)

    def begin(at, carry):
        other, _ = partner(me, at, n_exp, n_tile)
        pick(other)
        transfer(picked, returned, me, other, capacity, n_tile, send_sem, recv_sem)
        return carry

    lax.fori_loop(1, devices, begin, 0)

    def unwarp(other, origin):
        for rank in range(capacity):
            spot = other * capacity + rank
            which = ident[other, rank]
            back = lax.dot_general(
                warp_rows[which],
                origin[spot],
                (((0,), (0,)), ((), ())),
                preferred_element_type=jnp.float32,
            ).astype(jnp.bfloat16)
            piece = jnp.dot(back, warp_columns[which], preferred_element_type=jnp.float32)
            unwarped[spot] = piece.astype(unwarped.dtype)

    unwarp(me, picked)

    def finish(at, carry):
        _, other = partner(me, at, n_exp, n_tile)
        receipt(picked, returned, other, capacity, n_tile, send_sem, recv_sem).wait()
        unwarp(other, returned)
        return carry

    lax.fori_loop(1, devices, finish, 0)

    def gather(at, carry):
        left = pl.multiple_of(at * BLOCK, BLOCK)
        for block in range(image.shape[0] // BLOCK):
            image[block * BLOCK : (block + 1) * BLOCK, pl.ds(left, BLOCK)] = unwarped[
                place[0, block * across + at]
            ]
        return carry

    lax.fori_loop(0, across, gather, 0)
    start_edges(image, above, below, edge_send, edge_recv)
    finish_edges(image, above, below, edge_send, edge_recv)


def coadd_kernel(n_tile, table, weight, arrived, patch_out, value, sums, total, patch, done):
    slots = SLOT_ROWS * SLOT_COLS
    capacity = arrived.shape[0] // table.shape[0]
    blank = jnp.zeros((BLOCK, BLOCK), jnp.float32)

    def clear(at, carry):
        sums[at] = blank
        total[at] = 0.0
        return carry

    lax.fori_loop(0, slots + 1, clear, 0, unroll=5)

    def add(at, carry):
        share = weight[lax.div(at, n_tile), lax.rem(at, n_tile)]
        for rank in range(capacity):
            slot = table[at, rank]
            sums[slot] = sums[slot] + arrived[at * capacity + rank].astype(jnp.float32)
            total[slot] = total[slot] + share
        return carry

    lax.fori_loop(0, table.shape[0], add, 0, unroll=2)

    def divide(at, carry):
        for column in range(SLOT_COLS):
            number = at * SLOT_COLS + column
            weights = jnp.maximum(jnp.full((1, BLOCK), total[number], jnp.float32), 1.0)
            mean = sums[number] * (1.0 / weights)
            patch[
                pl.ds(pl.multiple_of(at * BLOCK, BLOCK), BLOCK),
                column * BLOCK : (column + 1) * BLOCK,
            ] = mean
            value[number] = mean.astype(value.dtype)
        strip = pl.ds(pl.multiple_of(at * BLOCK, BLOCK), BLOCK)
        pltpu.make_async_copy(patch.at[strip], patch_out.at[strip], done).start()
        return carry

    lax.fori_loop(0, SLOT_ROWS, divide, 0)
    value[slots] = blank.astype(value.dtype)
    pltpu.make_async_copy(patch, patch_out, done).wait()


def difference_kernel(
    coef, above, image, below, row_bands, bands, exposure, difference_out, padded, passes,
    difference, done,
):
    cols = image.shape[1]
    row_stage(coef, above, image, below, row_bands, padded, passes)

    def step(at, carry):
        start = pl.multiple_of(at * WIDE, WIDE)
        matched = column_chunk(passes, bands, start)
        spot = pl.ds(start, WIDE)
        difference[:, spot] = exposure[:, spot].astype(jnp.float32) - matched
        pltpu.make_async_copy(difference.at[:, spot], difference_out.at[:, spot], done).start()
        return carry

    lax.fori_loop(0, cols // WIDE, step, 0, unroll=2)
    pltpu.make_async_copy(difference, difference_out, done).wait()


def scalars(count):
    return [pl.BlockSpec(memory_space=pltpu.SMEM)] * count


def vectors(count):
    return [pl.BlockSpec(memory_space=pltpu.VMEM)] * count


def far(count):
    return [pl.BlockSpec(memory_space=pltpu.HBM)] * count


def shards(
    exposure, row_taps, column_taps, basis_coef, warp_rows, warp_columns, warp_id, route_device,
    route_slot, weight,
):
    n_exp = lax.axis_size("exp")
    n_tile = lax.axis_size("tile")
    devices = n_exp * n_tile
    rows, cols = exposure.shape[1:]
    bases = row_taps.shape[0]
    blocks = (rows // BLOCK) * (cols // BLOCK)
    capacity = max(2, (2 * blocks + devices - 1) // devices)
    slots = SLOT_ROWS * SLOT_COLS
    buffered = devices * capacity
    mine = exposure[0]
    route = route_device.reshape(devices, blocks)
    slot = route_slot.reshape(devices, blocks)

    def shape(*dims, dtype=jnp.bfloat16):
        return jax.ShapeDtypeStruct(dims, dtype)

    def params(units, **more):
        return pltpu.CompilerParams(vmem_limit_bytes=units * 1024 * 1024, **more)

    buffer = shape(buffered, BLOCK, BLOCK)
    buffer_units = (2 * buffered * BLOCK * BLOCK) // (1024 * 1024)
    bank_units = (4 * warp_rows.size) // (1024 * 1024)
    image_units = (2 * rows * cols) // (1024 * 1024)
    work_units = (bases + 2) * image_units
    slot_units = (4 * slots * BLOCK * BLOCK) // (1024 * 1024)
    spare = 6
    tables = shape(devices, capacity, dtype=jnp.int32)
    edge = shape(RIM, cols)
    pair = [pltpu.SemaphoreType.DMA((2,)), pltpu.SemaphoreType.DMA((2,))]
    semaphores = [pltpu.SemaphoreType.DMA((devices,)), pltpu.SemaphoreType.DMA((devices,))]
    work = [
        pltpu.VMEM((rows + 2 * RIM, cols), jnp.bfloat16),
        pltpu.VMEM((bases, rows, cols + 2 * BLOCK), jnp.bfloat16),
    ]

    above, below, row_bands, bands, source, ident, place = pl.pallas_call(
        prepare_kernel,
        out_shape=(
            edge, edge, shape(bases * BLOCK, BLOCK + 2 * RIM), shape(bases, 2 * WIDE, WIDE),
            tables, tables, shape(1, blocks, dtype=jnp.int32),
        ),
        in_specs=far(1) + vectors(2) + far(2),
        out_specs=tuple(vectors(7)),
        scratch_shapes=pair + [
            pltpu.VMEM((devices, blocks), jnp.int32),
            pltpu.VMEM((devices, blocks), jnp.int32),
            pltpu.SemaphoreType.DMA((2,)),
        ],
        compiler_params=params(56, collective_id=2, has_side_effects=True),
    )(mine, row_taps, column_taps, route, warp_id.reshape(devices, blocks))
    matched = pl.pallas_call(
        match_kernel,
        out_shape=shape(blocks + 1, BLOCK, BLOCK),
        in_specs=scalars(1) + vectors(5),
        out_specs=pl.BlockSpec(memory_space=pltpu.VMEM),
        scratch_shapes=work,
        compiler_params=params(work_units + 2 * image_units + spare),
    )(basis_coef, above, mine, below, row_bands, bands)
    arrived, table = pl.pallas_call(
        functools.partial(send_kernel, n_exp, n_tile),
        out_shape=(buffer, tables),
        in_specs=scalars(3) + vectors(5),
        out_specs=tuple(vectors(2)),
        scratch_shapes=[pltpu.VMEM(buffer.shape, buffer.dtype)] + semaphores,
        compiler_params=params(
            2 * buffer_units + bank_units + image_units + spare, collective_id=0,
            has_side_effects=True,
        ),
    )(source, ident, weight, matched, warp_rows, warp_columns, route, slot)
    patch, value = pl.pallas_call(
        functools.partial(coadd_kernel, n_tile),
        out_shape=(
            shape(SLOT_ROWS * BLOCK, SLOT_COLS * BLOCK, dtype=jnp.float32),
            shape(slots + 1, BLOCK, BLOCK),
        ),
        in_specs=scalars(2) + vectors(1),
        out_specs=tuple(far(1) + vectors(1)),
        scratch_shapes=[
            pltpu.VMEM((slots + 1, BLOCK, BLOCK), jnp.float32),
            pltpu.SMEM((slots + 1,), jnp.float32),
            pltpu.VMEM((SLOT_ROWS * BLOCK, SLOT_COLS * BLOCK), jnp.float32),
            pltpu.SemaphoreType.DMA(()),
        ],
        compiler_params=params(buffer_units + 3 * slot_units + spare),
    )(table, weight, arrived)
    template, template_above, template_below = pl.pallas_call(
        functools.partial(return_kernel, n_exp, n_tile),
        out_shape=(shape(rows, cols), edge, edge),
        in_specs=scalars(3) + vectors(3),
        out_specs=tuple(vectors(3)),
        scratch_shapes=[pltpu.VMEM(buffer.shape, buffer.dtype)] * 3 + semaphores + pair,
        compiler_params=params(
            3 * buffer_units + bank_units + slot_units + image_units + spare, collective_id=1,
            has_side_effects=True,
        ),
    )(ident, place, table, value, warp_rows, warp_columns)
    difference = pl.pallas_call(
        difference_kernel,
        out_shape=shape(rows, cols, dtype=jnp.float32),
        in_specs=scalars(1) + vectors(6),
        out_specs=far(1)[0],
        scratch_shapes=work + [
            pltpu.VMEM((rows, cols), jnp.float32), pltpu.SemaphoreType.DMA(()),
        ],
        compiler_params=params(work_units + 4 * image_units + spare),
    )(basis_coef, template_above, template, template_below, row_bands, bands, mine)
    return patch, difference[None]


def solution(mesh):
    placed = (P("exp", "tile", None), P(), P(), P("exp", None), P(), P(), P(), P(), P(), P())
    return jax.shard_map(
        shards,
        mesh=mesh,
        in_specs=placed,
        out_specs=(P("exp", "tile"), P("exp", "tile", None)),
        check_vma=False,
    )
```

```python
import functools

import jax
import jax.numpy as jnp
from jax import lax
from jax.experimental import pallas as pl
from jax.experimental.pallas import tpu as pltpu
from jax.sharding import PartitionSpec as P

BLOCK = 128
HALF = 10
RIM = 16
WIDE = 2 * BLOCK
SLOT_ROWS = 8
SLOT_COLS = 8


def edge_copies(image, above, below, send_sem, recv_sem):
    rows = image.shape[0]
    row, tile, count = lax.axis_index("exp"), lax.axis_index("tile"), lax.axis_size("tile")
    onward = pltpu.make_async_remote_copy(
        src_ref=image.at[pl.ds(rows - RIM, RIM)],
        dst_ref=above,
        send_sem=send_sem.at[0],
        recv_sem=recv_sem.at[0],
        device_id=(row, lax.rem(tile + 1, count)),
        device_id_type=pl.DeviceIdType.MESH,
    )
    backward = pltpu.make_async_remote_copy(
        src_ref=image.at[pl.ds(0, RIM)],
        dst_ref=below,
        send_sem=send_sem.at[1],
        recv_sem=recv_sem.at[1],
        device_id=(row, lax.rem(tile + count - 1, count)),
        device_id_type=pl.DeviceIdType.MESH,
    )
    return onward, backward


def start_edges(image, above, below, send_sem, recv_sem):
    tile, count = lax.axis_index("tile"), lax.axis_size("tile")
    onward, backward = edge_copies(image, above, below, send_sem, recv_sem)

    @pl.when(tile < count - 1)
    def _():
        onward.start()

    @pl.when(tile > 0)
    def _():
        backward.start()

    @pl.when(tile == 0)
    def _():
        above[...] = jnp.zeros_like(above)

    @pl.when(tile == count - 1)
    def _():
        below[...] = jnp.zeros_like(below)


def finish_edges(image, above, below, send_sem, recv_sem):
    tile, count = lax.axis_index("tile"), lax.axis_size("tile")
    onward, backward = edge_copies(image, above, below, send_sem, recv_sem)

    @pl.when(tile < count - 1)
    def _():
        onward.wait_send()
        backward.wait_recv()

    @pl.when(tile > 0)
    def _():
        backward.wait_send()
        onward.wait_recv()


def banded(taps, basis, lag):
    total = jnp.zeros(lag.shape, jnp.float32)
    for tap in range(taps.shape[1]):
        value = jnp.broadcast_to(taps[basis : basis + 1, tap : tap + 1], lag.shape)
        total = jnp.where(lag == tap, value, total)
    return total.astype(jnp.bfloat16)


def ranked(hit):
    count = hit.shape[1]
    later = (
        lax.broadcasted_iota(jnp.int32, (count, count), 0)
        < lax.broadcasted_iota(jnp.int32, (count, count), 1)
    )
    ranks = jnp.dot(
        hit.astype(jnp.float32), later.astype(jnp.float32), preferred_element_type=jnp.float32
    )
    return ranks.astype(jnp.int32)


def by_rank(hit, ranks, values, none, shape):
    column = lax.broadcasted_iota(jnp.int32, shape, 1)
    filled = jnp.zeros(shape, jnp.int32)
    for rank in range(shape[1]):
        chosen = jnp.where(hit & (ranks == rank), values - none, 0)
        filled = jnp.where(column == rank, jnp.sum(chosen, axis=1, keepdims=True) + none, filled)
    return filled


def prepare_kernel(
    image, row_taps, column_taps, route_all, warp_all, above, below, row_bands, bands, source,
    ident, place, send_sem, recv_sem, route, warp_id, load_sem,
):
    row, tile, count = lax.axis_index("exp"), lax.axis_index("tile"), lax.axis_size("tile")
    me = row * count + tile
    load_route = pltpu.make_async_copy(route_all, route, load_sem.at[0])
    load_warp = pltpu.make_async_copy(warp_all, warp_id, load_sem.at[1])
    load_route.start()
    load_warp.start()
    barrier = pltpu.get_barrier_semaphore()

    @pl.when(tile < count - 1)
    def _():
        pl.semaphore_signal(
            barrier, inc=1, device_id=(row, lax.rem(tile + 1, count)),
            device_id_type=pl.DeviceIdType.MESH,
        )

    @pl.when(tile > 0)
    def _():
        pl.semaphore_signal(
            barrier, inc=1, device_id=(row, lax.rem(tile + count - 1, count)),
            device_id_type=pl.DeviceIdType.MESH,
        )

    bases = row_taps.shape[0]
    taps = row_taps[...].astype(jnp.float32)
    shape = (BLOCK, BLOCK + 2 * RIM)
    lag = lax.broadcasted_iota(jnp.int32, shape, 1) - lax.broadcasted_iota(jnp.int32, shape, 0)
    for basis in range(bases):
        row_bands[basis * BLOCK : (basis + 1) * BLOCK, :] = banded(
            taps, basis, lag - (RIM - HALF)
        )

    peers = jnp.minimum(tile, 1) + jnp.minimum(count - 1 - tile, 1)
    pl.semaphore_wait(barrier, peers)

    start_edges(image, above, below, send_sem, recv_sem)

    taps = column_taps[...].astype(jnp.float32)
    shape = (3 * BLOCK, BLOCK)
    lag = lax.broadcasted_iota(jnp.int32, shape, 0) - lax.broadcasted_iota(jnp.int32, shape, 1)
    bands[...] = jnp.zeros_like(bands)
    for basis in range(bases):
        band = banded(taps, basis, lag - (BLOCK - HALF))
        for side in range(WIDE // BLOCK):
            top = side * BLOCK
            bands[basis, top : top + 3 * BLOCK, top : top + BLOCK] = band

    load_route.wait()
    load_warp.wait()
    devices, blocks = route.shape
    capacity = source.shape[1]
    device = lax.broadcasted_iota(jnp.int32, (devices, blocks), 0)
    hit = jnp.broadcast_to(route[pl.ds(me, 1), :], (devices, blocks)) == device
    ranks = ranked(hit)
    number = lax.broadcasted_iota(jnp.int32, (devices, blocks), 1)
    source[...] = by_rank(hit, ranks, number, blocks, source.shape)
    mine = jnp.broadcast_to(warp_id[pl.ds(me, 1), :], (devices, blocks))
    ident[...] = by_rank(hit, ranks, mine, 0, ident.shape)
    place[...] = jnp.sum(jnp.where(hit, device * capacity + ranks, 0), axis=0, keepdims=True)

    finish_edges(image, above, below, send_sem, recv_sem)


def row_stage(coef, above, image, below, row_bands, padded, passes):
    bases = passes.shape[0]
    rows, cols = image.shape
    blocks = rows // BLOCK
    span = BLOCK + 2 * RIM
    padded[:RIM, :] = above[...]
    padded[RIM : RIM + rows, :] = image[...]
    padded[RIM + rows :, :] = below[...]
    edge = jnp.zeros((rows, BLOCK), passes.dtype)
    for basis in range(bases):
        passes[basis, :, :BLOCK] = edge
        passes[basis, :, BLOCK + cols :] = edge

    def step(at, carry):
        start = pl.multiple_of(at * WIDE, WIDE)
        for block in range(blocks):
            top = block * BLOCK
            sums = jnp.dot(
                row_bands[...],
                padded[top : top + span, pl.ds(start, WIDE)],
                preferred_element_type=jnp.float32,
            )
            for basis in range(bases):
                scaled = coef[0, basis] * sums[basis * BLOCK : (basis + 1) * BLOCK]
                passes[basis, top : top + BLOCK, pl.ds(start + BLOCK, WIDE)] = scaled.astype(
                    passes.dtype
                )
        return carry

    lax.fori_loop(0, cols // WIDE, step, 0, unroll=2)


def column_chunk(passes, column_bands, start):
    total = None
    for basis in range(passes.shape[0]):
        term = jnp.dot(
            passes[basis, :, pl.ds(start, 2 * WIDE)],
            column_bands[basis],
            preferred_element_type=jnp.float32,
        )
        total = term if total is None else total + term
    return total


def match_kernel(coef, above, image, below, row_bands, bands, matched, padded, passes):
    rows, cols = image.shape
    blocks = rows // BLOCK
    across = cols // BLOCK
    row_stage(coef, above, image, below, row_bands, padded, passes)
    matched[blocks * across] = jnp.zeros((BLOCK, BLOCK), matched.dtype)

    def step(at, carry):
        start = pl.multiple_of(at * WIDE, WIDE)
        chunk = column_chunk(passes, bands, start).astype(matched.dtype)
        for block in range(blocks):
            for side in range(WIDE // BLOCK):
                number = block * across + at * (WIDE // BLOCK) + side
                matched[number] = chunk[
                    block * BLOCK : (block + 1) * BLOCK, side * BLOCK : (side + 1) * BLOCK
                ]
        return carry

    lax.fori_loop(0, cols // WIDE, step, 0, unroll=2)


def partner(me, step, n_exp, n_tile):
    row, tile = lax.div(me, n_tile), lax.rem(me, n_tile)
    half = n_exp // 2
    phase = lax.div(step, 2 * n_tile)
    side = lax.rem(step, 2)
    first = jnp.maximum(1 - phase, 0)
    down = half + phase * (2 * side - 1) - first * (1 - side) * half
    across = lax.div(lax.rem(step, 2 * n_tile), 2)
    target = lax.rem(row + down, n_exp) * n_tile + lax.rem(tile + across, n_tile)
    origin = lax.rem(row + n_exp - down, n_exp) * n_tile + lax.rem(tile + n_tile - across, n_tile)
    return target, origin


def address(device, n_tile):
    return (lax.div(device, n_tile), lax.rem(device, n_tile))


def greet(me, devices, n_tile):
    barrier = pltpu.get_barrier_semaphore()

    def hello(step, carry):
        other = lax.rem(me + step + 1, devices)
        pl.semaphore_signal(
            barrier, inc=1, device_id=address(other, n_tile), device_id_type=pl.DeviceIdType.MESH
        )
        return carry

    lax.fori_loop(0, devices - 1, hello, 0)
    return barrier


def transfer(source, target, me, other, capacity, n_tile, send_sem, recv_sem):
    for rank in range(capacity):
        pltpu.make_async_remote_copy(
            src_ref=source.at[pl.ds(other * capacity + rank, 1)],
            dst_ref=target.at[pl.ds(me * capacity + rank, 1)],
            send_sem=send_sem.at[other],
            recv_sem=recv_sem.at[me],
            device_id=address(other, n_tile),
            device_id_type=pl.DeviceIdType.MESH,
        ).start()


def receipt(source, target, other, capacity, n_tile, send_sem, recv_sem):
    return pltpu.make_async_remote_copy(
        src_ref=source.at[pl.ds(other * capacity, capacity)],
        dst_ref=target.at[pl.ds(other * capacity, capacity)],
        send_sem=send_sem.at[other],
        recv_sem=recv_sem.at[other],
        device_id=address(other, n_tile),
        device_id_type=pl.DeviceIdType.MESH,
    )


def send_kernel(
    n_exp, n_tile, source, ident, weight, matched, warp_rows, warp_columns, route, slot, arrived,
    table, packed, send_sem, recv_sem,
):
    devices = n_exp * n_tile
    capacity = packed.shape[0] // devices
    me = lax.axis_index("exp") * n_tile + lax.axis_index("tile")
    barrier = greet(me, devices, n_tile)
    scale = weight[lax.axis_index("exp"), lax.axis_index("tile")]

    def warp(other, target):
        for rank in range(capacity):
            spot = other * capacity + rank
            which = ident[other, rank]
            first = jnp.dot(
                warp_rows[which], matched[source[other, rank]], preferred_element_type=jnp.float32
            ).astype(jnp.bfloat16)
            second = lax.dot_general(
                first,
                warp_columns[which],
                (((1,), (1,)), ((), ())),
                preferred_element_type=jnp.float32,
            )
            target[spot] = (scale * second).astype(target.dtype)

    warp(me, arrived)
    pl.semaphore_wait(barrier, devices - 1)

    def step(at, carry):
        other, _ = partner(me, at, n_exp, n_tile)
        warp(other, packed)
        transfer(packed, arrived, me, other, capacity, n_tile, send_sem, recv_sem)
        return carry

    lax.fori_loop(1, devices, step, 0)

    hit = route[...] == me
    table[...] = by_rank(hit, ranked(hit), slot[...], SLOT_ROWS * SLOT_COLS, table.shape)

    def finish(at, carry):
        _, other = partner(me, at, n_exp, n_tile)
        receipt(packed, arrived, other, capacity, n_tile, send_sem, recv_sem).wait()
        return carry

    lax.fori_loop(1, devices, finish, 0)


def return_kernel(
    n_exp, n_tile, ident, place, table, value, warp_rows, warp_columns, image, above, below,
    picked, returned, unwarped, send_sem, recv_sem, edge_send, edge_recv,
):
    devices = n_exp * n_tile
    capacity = picked.shape[0] // devices
    across = image.shape[1] // BLOCK
    me = lax.axis_index("exp") * n_tile + lax.axis_index("tile")
    barrier = greet(me, devices, n_tile)

    def pick(other):
        for rank in range(capacity):
            picked[other * capacity + rank] = value[table[other, rank]]

    pick(me)
    pl.semaphore_wait(barrier, devices - 1)

    def begin(at, carry):
        other, _ = partner(me, at, n_exp, n_tile)
        pick(other)
        transfer(picked, returned, me, other, capacity, n_tile, send_sem, recv_sem)
        return carry

    lax.fori_loop(1, devices, begin, 0)

    def unwarp(other, origin):
        for rank in range(capacity):
            spot = other * capacity + rank
            which = ident[other, rank]
            back = lax.dot_general(
                warp_rows[which],
                origin[spot],
                (((0,), (0,)), ((), ())),
                preferred_element_type=jnp.float32,
            ).astype(jnp.bfloat16)
            piece = jnp.dot(back, warp_columns[which], preferred_element_type=jnp.float32)
            unwarped[spot] = piece.astype(unwarped.dtype)

    unwarp(me, picked)

    def finish(at, carry):
        _, other = partner(me, at, n_exp, n_tile)
        receipt(picked, returned, other, capacity, n_tile, send_sem, recv_sem).wait()
        unwarp(other, returned)
        return carry

    lax.fori_loop(1, devices, finish, 0)

    def gather(at, carry):
        left = pl.multiple_of(at * BLOCK, BLOCK)
        for block in range(image.shape[0] // BLOCK):
            image[block * BLOCK : (block + 1) * BLOCK, pl.ds(left, BLOCK)] = unwarped[
                place[0, block * across + at]
            ]
        return carry

    lax.fori_loop(0, across, gather, 0)
    start_edges(image, above, below, edge_send, edge_recv)
    finish_edges(image, above, below, edge_send, edge_recv)


def coadd_kernel(n_tile, table, weight, arrived, patch_out, value, sums, total, patch, done):
    slots = SLOT_ROWS * SLOT_COLS
    capacity = arrived.shape[0] // table.shape[0]
    blank = jnp.zeros((BLOCK, BLOCK), jnp.float32)

    def clear(at, carry):
        sums[at] = blank
        total[at] = 0.0
        return carry

    lax.fori_loop(0, slots + 1, clear, 0, unroll=5)

    def add(at, carry):
        share = weight[lax.div(at, n_tile), lax.rem(at, n_tile)]
        for rank in range(capacity):
            slot = table[at, rank]
            sums[slot] = sums[slot] + arrived[at * capacity + rank].astype(jnp.float32)
            total[slot] = total[slot] + share
        return carry

    lax.fori_loop(0, table.shape[0], add, 0, unroll=2)

    def divide(at, carry):
        for column in range(SLOT_COLS):
            number = at * SLOT_COLS + column
            weights = jnp.maximum(jnp.full((1, BLOCK), total[number], jnp.float32), 1.0)
            mean = sums[number] * (1.0 / weights)
            patch[
                pl.ds(pl.multiple_of(at * BLOCK, BLOCK), BLOCK),
                column * BLOCK : (column + 1) * BLOCK,
            ] = mean
            value[number] = mean.astype(value.dtype)
        strip = pl.ds(pl.multiple_of(at * BLOCK, BLOCK), BLOCK)
        pltpu.make_async_copy(patch.at[strip], patch_out.at[strip], done).start()
        return carry

    lax.fori_loop(0, SLOT_ROWS, divide, 0)
    value[slots] = blank.astype(value.dtype)
    pltpu.make_async_copy(patch, patch_out, done).wait()


def difference_kernel(
    coef, above, image, below, row_bands, bands, exposure, difference_out, padded, passes,
    difference, done,
):
    cols = image.shape[1]
    row_stage(coef, above, image, below, row_bands, padded, passes)

    def step(at, carry):
        start = pl.multiple_of(at * WIDE, WIDE)
        matched = column_chunk(passes, bands, start)
        spot = pl.ds(start, WIDE)
        difference[:, spot] = exposure[:, spot].astype(jnp.float32) - matched
        pltpu.make_async_copy(difference.at[:, spot], difference_out.at[:, spot], done).start()
        return carry

    lax.fori_loop(0, cols // WIDE, step, 0, unroll=2)
    pltpu.make_async_copy(difference, difference_out, done).wait()


def scalars(count):
    return [pl.BlockSpec(memory_space=pltpu.SMEM)] * count


def vectors(count):
    return [pl.BlockSpec(memory_space=pltpu.VMEM)] * count


def far(count):
    return [pl.BlockSpec(memory_space=pltpu.HBM)] * count


def shards(
    exposure, row_taps, column_taps, basis_coef, warp_rows, warp_columns, warp_id, route_device,
    route_slot, weight,
):
    n_exp = lax.axis_size("exp")
    n_tile = lax.axis_size("tile")
    devices = n_exp * n_tile
    rows, cols = exposure.shape[1:]
    bases = row_taps.shape[0]
    blocks = (rows // BLOCK) * (cols // BLOCK)
    capacity = max(2, (2 * blocks + devices - 1) // devices)
    slots = SLOT_ROWS * SLOT_COLS
    buffered = devices * capacity
    mine = exposure[0]
    route = route_device.reshape(devices, blocks)
    slot = route_slot.reshape(devices, blocks)

    def shape(*dims, dtype=jnp.bfloat16):
        return jax.ShapeDtypeStruct(dims, dtype)

    def params(units, **more):
        return pltpu.CompilerParams(vmem_limit_bytes=units * 1024 * 1024, **more)

    buffer = shape(buffered, BLOCK, BLOCK)
    buffer_units = (2 * buffered * BLOCK * BLOCK) // (1024 * 1024)
    bank_units = (4 * warp_rows.size) // (1024 * 1024)
    image_units = (2 * rows * cols) // (1024 * 1024)
    work_units = (bases + 2) * image_units
    slot_units = (4 * slots * BLOCK * BLOCK) // (1024 * 1024)
    spare = 6
    tables = shape(devices, capacity, dtype=jnp.int32)
    edge = shape(RIM, cols)
    pair = [pltpu.SemaphoreType.DMA((2,)), pltpu.SemaphoreType.DMA((2,))]
    semaphores = [pltpu.SemaphoreType.DMA((devices,)), pltpu.SemaphoreType.DMA((devices,))]
    work = [
        pltpu.VMEM((rows + 2 * RIM, cols), jnp.bfloat16),
        pltpu.VMEM((bases, rows, cols + 2 * BLOCK), jnp.bfloat16),
    ]

    above, below, row_bands, bands, source, ident, place = pl.pallas_call(
        prepare_kernel,
        out_shape=(
            edge, edge, shape(bases * BLOCK, BLOCK + 2 * RIM), shape(bases, 2 * WIDE, WIDE),
            tables, tables, shape(1, blocks, dtype=jnp.int32),
        ),
        in_specs=far(1) + vectors(2) + far(2),
        out_specs=tuple(vectors(7)),
        scratch_shapes=pair + [
            pltpu.VMEM((devices, blocks), jnp.int32),
            pltpu.VMEM((devices, blocks), jnp.int32),
            pltpu.SemaphoreType.DMA((2,)),
        ],
        compiler_params=params(spare + 4, collective_id=2, has_side_effects=True),
    )(mine, row_taps, column_taps, route, warp_id.reshape(devices, blocks))
    matched = pl.pallas_call(
        match_kernel,
        out_shape=shape(blocks + 1, BLOCK, BLOCK),
        in_specs=scalars(1) + vectors(5),
        out_specs=pl.BlockSpec(memory_space=pltpu.VMEM),
        scratch_shapes=work,
        compiler_params=params(work_units + 2 * image_units + spare),
    )(basis_coef, above, mine, below, row_bands, bands)
    arrived, table = pl.pallas_call(
        functools.partial(send_kernel, n_exp, n_tile),
        out_shape=(buffer, tables),
        in_specs=scalars(3) + vectors(5),
        out_specs=tuple(vectors(2)),
        scratch_shapes=[pltpu.VMEM(buffer.shape, buffer.dtype)] + semaphores,
        compiler_params=params(
            2 * buffer_units + bank_units + image_units + spare, collective_id=0,
            has_side_effects=True,
        ),
    )(source, ident, weight, matched, warp_rows, warp_columns, route, slot)
    patch, value = pl.pallas_call(
        functools.partial(coadd_kernel, n_tile),
        out_shape=(
            shape(SLOT_ROWS * BLOCK, SLOT_COLS * BLOCK, dtype=jnp.float32),
            shape(slots + 1, BLOCK, BLOCK),
        ),
        in_specs=scalars(2) + vectors(1),
        out_specs=tuple(far(1) + vectors(1)),
        scratch_shapes=[
            pltpu.VMEM((slots + 1, BLOCK, BLOCK), jnp.float32),
            pltpu.SMEM((slots + 1,), jnp.float32),
            pltpu.VMEM((SLOT_ROWS * BLOCK, SLOT_COLS * BLOCK), jnp.float32),
            pltpu.SemaphoreType.DMA(()),
        ],
        compiler_params=params(buffer_units + 3 * slot_units + spare),
    )(table, weight, arrived)
    template, template_above, template_below = pl.pallas_call(
        functools.partial(return_kernel, n_exp, n_tile),
        out_shape=(shape(rows, cols), edge, edge),
        in_specs=scalars(3) + vectors(3),
        out_specs=tuple(vectors(3)),
        scratch_shapes=[pltpu.VMEM(buffer.shape, buffer.dtype)] * 3 + semaphores + pair,
        compiler_params=params(
            3 * buffer_units + bank_units + slot_units + image_units + spare, collective_id=1,
            has_side_effects=True,
        ),
    )(ident, place, table, value, warp_rows, warp_columns)
    difference = pl.pallas_call(
        difference_kernel,
        out_shape=shape(rows, cols, dtype=jnp.float32),
        in_specs=scalars(1) + vectors(6),
        out_specs=far(1)[0],
        scratch_shapes=work + [
            pltpu.VMEM((rows, cols), jnp.float32), pltpu.SemaphoreType.DMA(()),
        ],
        compiler_params=params(work_units + 4 * image_units + spare),
    )(basis_coef, template_above, template, template_below, row_bands, bands, mine)
    return patch, difference[None]


def solution(mesh):
    placed = (P("exp", "tile", None), P(), P(), P("exp", None), P(), P(), P(), P(), P(), P())
    return jax.shard_map(
        shards,
        mesh=mesh,
        in_specs=placed,
        out_specs=(P("exp", "tile"), P("exp", "tile", None)),
        check_vma=False,
    )
```
